512 devices in a mesh: ty: 16 (over z, core), tx: 32 (over x, y).
Axes of the slice: x: 4, y: 8, z: 8, core: 2. Of those that a mesh axis runs over, the one named last changes fastest.
Arguments:
- points: float32 [16, 32, 3, 4096], P('ty', 'tx'), may hold values from 0 to 64
- probes: float32 [16, 32, 8, 4096], P('ty', 'tx'), may hold values from -0.6 to 0.6
- near_boxes: int32 [16, 32, 16, 27], P('ty', 'tx'), may hold values from -1 to 8191, as said below
- leaf_bases: float32 [16, 32, 64, 4096], P('ty', 'tx'), may hold values from -0.375 to 0.375
- box_transfer: float32 [16, 32, 16, 64, 64], P('ty', 'tx'), may hold values from -1 to 1
- upper_transfer: float32 [9, 2, 64, 64], replicated, may hold values from -1 to 1
Outputs:
- near_field: float32 [16, 32, 8, 4096], P('ty', 'tx')
- leaf_factor: float32 [16, 32, 16, 64, 64], P('ty', 'tx')
- ancestors: float32 [16, 32, 10, 64, 64], P('ty', 'tx')
The draws below stay inside these ranges and needn't reach their ends.
Inputs may be any that keep to these rules, and one draw needn't show every extreme that they name: `near_boxes`: box k of tile (ty, tx) sits at grid cell (2 ty + k % 2, 2 tx + (k // 2) % 2, k // 4). Slot s of a box's list names the box at cell offset (s // 9 - 1, (s // 3) % 3 - 1, s % 3 - 1) from it, or -1; slot 13 names the box itself. Every named box lies in the box's own tile or one of the eight tiles around it.
All inputs are finite; a program needn't handle non-finite values.
Results may differ from the reference program's by a relative error of at most 0.004.
Values sent between devices are 32-bit elements; how exact they have to be, the bound alone decides.
A program may use at most 64 MiB of HBM per device.

```python
import jax
import jax.numpy as jnp
from jax import lax

BOX_DEV = 16
BOX_PTS = 256
RANK = 64
PROBES = 8
NEAR = 27
LOG_TX = 5
LOG_TY = 4
LEVELS = 9
BOXES = 8192
N_TY = 16
N_TX = 32


def draw_points(key, part):
    key = jax.random.fold_in(key, 11)
    row_width = BOX_DEV * BOX_PTS
    box_k = jnp.arange(row_width, dtype=jnp.int32) // BOX_PTS
    tile_row = jnp.arange(N_TY, dtype=jnp.int32)[:, None, None]
    tile_col = jnp.arange(N_TX, dtype=jnp.int32)[None, :, None]
    corner_x = jnp.broadcast_to(2 * tile_row + box_k[None, None, :] % 2, (N_TY, N_TX, row_width))
    corner_y = jnp.broadcast_to(2 * tile_col + box_k[None, None, :] // 2 % 2, (N_TY, N_TX, row_width))
    corner_z = jnp.broadcast_to(box_k[None, None, :] // 4, (N_TY, N_TX, row_width))
    corner = jnp.stack([corner_x, corner_y, corner_z], axis=2).astype(jnp.float32)
    offset = jax.random.uniform(key, (N_TY, N_TX, 3, row_width), jnp.float32)
    return corner + offset


def draw_near_boxes(key, part):
    key = jax.random.fold_in(key, 23)
    tile_row = jnp.arange(N_TY, dtype=jnp.int32)[:, None, None, None]
    tile_col = jnp.arange(N_TX, dtype=jnp.int32)[None, :, None, None]
    box_k = jnp.arange(BOX_DEV, dtype=jnp.int32)[None, None, :, None]
    slot_s = jnp.arange(NEAR, dtype=jnp.int32)[None, None, None, :]
    grid_x = 2 * tile_row + box_k % 2 + slot_s // 9 - 1
    grid_y = 2 * tile_col + box_k // 2 % 2 + slot_s // 3 % 3 - 1
    grid_z = box_k // 4 + slot_s % 3 - 1
    inside = (grid_x >= 0) & (grid_x < 2 * N_TY) & (grid_y >= 0) & (grid_y < 2 * N_TX) & (grid_z >= 0) & (grid_z < BOX_DEV // 4)
    safe_x = jnp.clip(grid_x, 0, 2 * N_TY - 1)
    safe_y = jnp.clip(grid_y, 0, 2 * N_TX - 1)
    safe_z = jnp.clip(grid_z, 0, BOX_DEV // 4 - 1)
    ident = (safe_x // 2 * N_TX + safe_y // 2) * BOX_DEV + safe_x % 2 + 2 * (safe_y % 2) + 4 * safe_z
    shape = (N_TY, N_TX, BOX_DEV, NEAR)
    keep = (jax.random.randint(key, shape, 0, 4) > 0) | (slot_s == 13)
    return jnp.where(inside & keep, ident, -1).astype(jnp.int32)


def draw_box_transfer(key, part):
    key = jax.random.fold_in(key, 37)
    noise = jax.random.uniform(key, (N_TY, N_TX, BOX_DEV, RANK, RANK), jnp.float32, -1.0, 1.0)
    eye = jnp.eye(RANK, dtype=jnp.float32)
    return (eye + noise * (0.5 / RANK ** 0.5)) / BOX_DEV ** 0.5


def draw_upper_transfer(key, part):
    key = jax.random.fold_in(key, 41)
    noise = jax.random.uniform(key, (LEVELS, 2, RANK, RANK), jnp.float32, -1.0, 1.0)
    eye = jnp.eye(RANK, dtype=jnp.float32)
    return 0.7 * eye + noise * (0.35 / RANK ** 0.5)


def level_of(key, shape, pieces, smallest, top_value):
    factor_of, own = 1.0, jax.random.fold_in(key, 6)
    for dim, shards_of in pieces:
        draws = jnp.exp(jax.random.uniform(jax.random.fold_in(own, dim), (shards_of,), jnp.float32, smallest / len(pieces), top_value / len(pieces)))
        factor_of = factor_of * jnp.repeat(draws, shape[dim] // shards_of).reshape([-1 if axis == dim else 1 for axis in range(len(shape))])
    return factor_of


def gaussian(stream_key, shape, spread, bound, shards=(), kind=jnp.bfloat16):
    level = level_of(stream_key, shape, shards, -0.22, 0.18) if shards else 1.0
    values = jax.random.normal(stream_key, shape, jnp.float32) * spread * level
    return jnp.minimum(jnp.maximum(values, -bound), bound).astype(kind)


def setup_inputs(seed: int = 0) -> dict:
    key_list = jax.random.split(jax.random.key(seed), 7)
    return {
        "points": draw_points(jax.random.fold_in(key_list[6], 71), 0),
        "probes": gaussian(key_list[1], (N_TY, N_TX, PROBES, BOX_DEV * BOX_PTS), 0.1, 0.6, ((0, 16), (1, 32)), jnp.float32),
        "near_boxes": draw_near_boxes(jax.random.fold_in(key_list[6], 71), 0),
        "leaf_bases": gaussian(key_list[3], (N_TY, N_TX, RANK, BOX_DEV * BOX_PTS), BOX_PTS ** -0.5, 0.375, ((0, 16), (1, 32)), jnp.float32),
        "box_transfer": draw_box_transfer(jax.random.fold_in(key_list[6], 71), 0),
        "upper_transfer": draw_upper_transfer(jax.random.fold_in(key_list[6], 71), 0),
    }


length_scale = 1.0
root_three = 1.7320508075688772

def kernel_block(target, source):
    dist_sq = jnp.zeros((source.shape[0], target.shape[1], source.shape[2]), jnp.float32)
    for coord in range(3):
        delta = target[coord][None, :, None] - source[:, coord][:, None, :]
        dist_sq = dist_sq + delta * delta
    scaled = root_three * jnp.sqrt(dist_sq) / length_scale
    return ((1.0 + scaled) * jnp.exp(-scaled)).astype(jnp.bfloat16)

def upper_factor(gram_sum):
    return jnp.swapaxes(jnp.linalg.cholesky(gram_sum), -1, -2)

def merge_pair(left_node, right_node, transfers):
    left_term = jnp.matmul(left_node, transfers[0], precision=lax.Precision.HIGHEST)
    right_term = jnp.matmul(right_node, transfers[1], precision=lax.Precision.HIGHEST)
    gram_sum = jnp.matmul(jnp.swapaxes(left_term, -1, -2), left_term, precision=lax.Precision.HIGHEST)
    gram_sum = gram_sum + jnp.matmul(jnp.swapaxes(right_term, -1, -2), right_term, precision=lax.Precision.HIGHEST)
    return upper_factor(gram_sum)

def reference(points, probes, near_boxes, leaf_bases, box_transfer, upper_transfer):
    row_width = BOX_DEV * BOX_PTS
    all_points = points.reshape(N_TY, N_TX, 3, BOX_DEV, BOX_PTS).transpose(0, 1, 3, 2, 4).reshape(BOXES, 3, BOX_PTS)
    rounded = probes.astype(jnp.bfloat16)
    all_probes = rounded.reshape(N_TY, N_TX, PROBES, BOX_DEV, BOX_PTS).transpose(0, 1, 3, 2, 4).reshape(BOXES, PROBES, BOX_PTS)
    slot_table = near_boxes.reshape(BOXES, NEAR)

    def per_box(packed):
        target, slot_ids = packed
        is_valid = slot_ids >= 0
        safe_ids = jnp.where(is_valid, slot_ids, 0).astype(jnp.int32)
        source_pts = all_points[safe_ids]
        source_prb = all_probes[safe_ids] * is_valid[:, None, None].astype(jnp.bfloat16)
        kernel = kernel_block(target, source_pts)
        return jnp.einsum('kts,kcs->ct', kernel.astype(jnp.float32), source_prb.astype(jnp.float32), precision=lax.Precision.HIGHEST)
    near_out = lax.map(per_box, (all_points, slot_table))
    near_field = near_out.reshape(N_TY, N_TX, BOX_DEV, PROBES, BOX_PTS).transpose(0, 1, 3, 2, 4).reshape(N_TY, N_TX, PROBES, row_width)
    basis_view = leaf_bases.reshape(N_TY, N_TX, RANK, BOX_DEV, BOX_PTS)
    leaf_gram = jnp.einsum('yxrbp,yxsbp->yxbrs', basis_view, basis_view, precision=lax.Precision.HIGHEST)
    leaf_factor = upper_factor(leaf_gram)
    stacked = jnp.einsum('yxbrs,yxbst->yxbrt', leaf_factor, box_transfer, precision=lax.Precision.HIGHEST)
    tile_gram = jnp.einsum('yxbrt,yxbru->yxtu', stacked, stacked, precision=lax.Precision.HIGHEST)
    current = upper_factor(tile_gram)
    history = [current]
    level_idx = 0
    for bit_pos in range(LOG_TX):
        paired = current.reshape(N_TY, -1, 2, RANK, RANK)
        current = merge_pair(paired[:, :, 0], paired[:, :, 1], upper_transfer[level_idx])
        history.append(jnp.repeat(current, 2 ** (bit_pos + 1), axis=1))
        level_idx = level_idx + 1
    for bit_pos in range(LOG_TY):
        paired = current.reshape(-1, 2, 1, RANK, RANK)
        current = merge_pair(paired[:, 0], paired[:, 1], upper_transfer[level_idx])
        history.append(jnp.repeat(jnp.repeat(current, 2 ** (bit_pos + 1), axis=0), N_TX, axis=1))
        level_idx = level_idx + 1
    ancestors = jnp.stack(history, axis=2)
    return (near_field, leaf_factor, ancestors)
```

```python
import functools
import math

import jax
import jax.numpy as jnp
from jax import lax
from jax.experimental import pallas as pl
from jax.experimental.pallas import tpu as pltpu
from jax.sharding import PartitionSpec as P

MESH = pl.DeviceIdType.MESH
HIGHEST = lax.Precision.HIGHEST
F32, BF16 = jnp.float32, jnp.bfloat16
LN2 = math.log(2.0)
ALPHA = math.sqrt(3.0) / LN2
BOXES, PTS, RANK = 16, 256, 64
COLUMNS = ((0, 1), (0, 0), (1, 0), (1, 1))
BOX_AT = tuple(x + 2 * y + 4 * z for x, y in COLUMNS for z in range(4))
HALO = ((0, -1, 4, 8, 0), (-1, 0, 0, 8, 8), (-1, -1, 4, 4, 16), (-1, 1, 0, 4, 20))
REMOTE = 24
Z_PAIRS = tuple((a, b) for a in range(4) for b in range(4) if abs(a - b) <= 1)


def dot(a, b, ca, cb, precision=None):
    return lax.dot_general(
        a, b, (((ca,), (cb,)), ((), ())), precision=precision, preferred_element_type=F32
    )


def split3(value):
    high = value.astype(BF16).astype(F32)
    rest = value - high
    mid = rest.astype(BF16).astype(F32)
    return high, mid, (rest - mid).astype(BF16).astype(F32)


def features(rows, center, left):
    sub = lax.broadcasted_iota(jnp.int32, rows.shape, 0)
    cy, cx = center
    mid = jnp.where(sub == 0, cy, jnp.where(sub == 1, cx, 2.0))
    y = jnp.where(sub < 3, (rows - mid) * ALPHA, 0.0)
    norm = jnp.sum(y * y, axis=0, keepdims=True)
    zero = jnp.zeros_like(y)
    if left:
        h, m, l = split3(jnp.where(sub == 3, norm, y))
        one = jnp.where(sub == 4, 1.0, 0.0)
        coord = lambda v: jnp.where(sub < 3, -2.0 * v, 0.0)
        lead = lambda c, n: jnp.where(sub < 3, -2.0 * c, jnp.where(sub == 3, n, one))
        parts = (lead(h, h), lead(h, m), lead(m, l), coord(m), coord(h), coord(l))
    else:
        h, m, l = split3(jnp.where(sub == 4, norm, y))
        one = jnp.where(sub == 3, 1.0, 0.0)
        parts = (h + one, m + one, jnp.where(sub < 3, h, l) + one, m, l, h)
    return jnp.concatenate(parts, axis=0).astype(BF16)


def matern(square):
    s = jnp.maximum(square, 1e-12)
    u = s * lax.rsqrt(s)
    return ((1.0 + LN2 * u) * jnp.exp2(-u)).astype(BF16)


def halves(packed):
    return jnp.concatenate([packed[:, :RANK], packed[:, RANK:]], axis=0)


def packed(full):
    return jnp.concatenate([full[:32], full[32:]], axis=1)


def remote(src, dst, send, recv, device, comm):
    if comm:
        return pltpu.make_async_remote_copy(
            src_ref=src, dst_ref=dst, send_sem=send, recv_sem=recv, device_id=device, device_id_type=MESH
        )
    return None


def main_kernel(sizes, comm, pts, prb, near, leaf, trans, upper, near_out, gram_out,
                box, left, right, mask, acc, back, kern, grams, tree_out, tree_in,
                halo_send, halo_recv, back_send, back_recv, tree_send, tree_recv):
    n_ty, n_tx = sizes
    ty, tx = (lax.axis_index("ty"), lax.axis_index("tx")) if comm else (jnp.int32(0), jnp.int32(0))
    center = ((2 * ty + 1).astype(F32), (2 * tx + 1).astype(F32))

    def at(dy, dx):
        return (lax.rem(ty + dy + n_ty, n_ty), lax.rem(tx + dx + n_tx, n_tx))

    bits = [lax.rem(tx // 2**i, 2) for i in range(5)] + [lax.rem(ty // 2**i, 2) for i in range(4)]

    def relative(level, q):
        row, col = ty, tx
        for i in range(3):
            if q >> i & 1:
                b = level + i
                if b < 5:
                    col = col + 2**b * (1 - 2 * bits[b])
                else:
                    row = row + 2 ** (b - 5) * (1 - 2 * bits[b])
        return (row, col)

    peers = [at(*h[:2]) for h in HALO] + [at(-h[0], -h[1]) for h in HALO]
    peers += [relative(3 * r, q) for r in range(3) for q in range(1, 8)]
    if comm:
        barrier = pltpu.get_barrier_semaphore()
        for peer in peers:
            pl.semaphore_signal(barrier, inc=1, device_id=peer, device_id_type=MESH)

    for i, k in enumerate(BOX_AT):
        cols = slice(k * PTS, (k + 1) * PTS)
        box[i, 0:3, :] = pts[0, 0, :, cols]
        box[i, 8:16, :] = prb[0, 0, :, cols]
        box[i, 3:8, :] = jnp.zeros((5, PTS), F32)
        box[i, 3:4, 0:27] = jnp.where(near[0, 0, k : k + 1, :] >= 0, 1.0, 0.0)

    if comm:
        pl.semaphore_wait(barrier, len(peers))

    def halo(j):
        dy, dx, first, count, row = HALO[j]
        src, dst = box.at[pl.ds(first, count)], box.at[pl.ds(BOXES + row, count)]
        if comm:
            return pltpu.make_async_remote_copy(
                src_ref=src, dst_ref=dst, send_sem=halo_send.at[j], recv_sem=halo_recv.at[j],
                device_id=at(dy, dx), device_id_type=MESH)
        return pltpu.make_async_copy(src, dst, halo_recv.at[j])

    def reply(j):
        dy, dx, first, count, row = HALO[j]
        src, dst = acc.at[pl.ds(BOXES + row, count)], back.at[pl.ds(row, count)]
        if comm:
            return pltpu.make_async_remote_copy(
                src_ref=src, dst_ref=dst, send_sem=back_send.at[j], recv_sem=back_recv.at[j],
                device_id=at(-dy, -dx), device_id_type=MESH)
        return pltpu.make_async_copy(src, dst, back_recv.at[j])

    def exchange(r, q):
        count = 3 if q == 1 else 2 if q < 4 else 1
        src, dst = tree_out.at[r, pl.ds(0, count)], tree_in.at[r, q - 1, pl.ds(0, count)]
        j = 7 * r + q - 1
        if comm:
            return pltpu.make_async_remote_copy(
                src_ref=src, dst_ref=dst, send_sem=tree_send.at[j], recv_sem=tree_recv.at[j],
                device_id=relative(3 * r, q), device_id_type=MESH)
        return pltpu.make_async_copy(src, dst, tree_recv.at[j])

    def wait_send(copy):
        if comm:
            copy.wait_send()

    def wait_recv(copy):
        if comm:
            copy.wait_recv()
        else:
            copy.wait()

    for j in range(4):
        halo(j).start()

    total = jnp.zeros((RANK, RANK), F32)
    pair = []
    for k in range(BOXES):
        v = leaf[0, 0, :, k * PTS : (k + 1) * PTS]
        stack = jnp.concatenate(split3(v), axis=0).astype(BF16)
        c = dot(stack, stack, 1, 1)
        g = c[128:, :64] + c[:64, 128:] + c[64:128, 64:128]
        g = g + (c[:64, 64:128] + c[64:128, :64]) + c[:64, :64]
        pair.append(g)
        if k % 2:
            gram_out[k // 2] = jnp.concatenate(pair, axis=1)
            pair = []
        t = trans[0, 0, k]
        total = total + dot(t, dot(g, t, 1, 0, HIGHEST), 0, 0, HIGHEST)
    grams[0] = total

    def send_round(r):
        node = grams[3 * r]
        path = None
        for i in range(3):
            step = upper[3 * r + i, bits[3 * r + i]]
            path = step if path is None else dot(path, step, 1, 0, HIGHEST)
            term = dot(path, dot(node, path, 1, 0, HIGHEST), 0, 0, HIGHEST)
            tree_out[r, 2 - i] = packed(term)
        for q in range(1, 8):
            exchange(r, q).start()

    def finish_round(r):
        for q in range(1, 8):
            wait_recv(exchange(r, q))
        for i in range(3):
            node = tree_out[r, 2 - i]
            for q in range(1, 2 ** (i + 1)):
                node = node + tree_in[r, q - 1, 2 - i]
            grams[3 * r + i + 1] = halves(node)

    send_round(0)

    lane = lax.broadcasted_iota(jnp.int32, (32, 128), 1)
    row = lax.broadcasted_iota(jnp.int32, (32, 128), 0)
    ones = jnp.ones((128, 128), BF16)
    diag = lax.broadcasted_iota(jnp.int32, (PTS, PTS), 0) == lax.broadcasted_iota(jnp.int32, (PTS, PTS), 1)
    eye = jnp.where(diag, 1.0, 0.0).astype(BF16)

    def prepare(i, own):
        rows = box[i, 0:8, :]
        right[i] = features(rows, center, False)
        if own:
            left[i] = dot(eye, features(rows, center, True), 1, 1).astype(BF16)
        slots = jnp.where(lane == row, box[i, 3:4, 0:128], 0.0).astype(BF16)
        mask[i] = dot(slots, ones, 1, 0)
        acc[i] = jnp.zeros((8, PTS), F32)

    def loop(n, body):
        lax.fori_loop(0, n, lambda i, c: (body(i), c)[1], 0)

    def probe(i, owner, slot):
        m = mask[owner, pl.ds(slot, 1), :]
        return (box[i, 8:16, :] * jnp.concatenate([m, m], axis=1)).astype(BF16)

    def blocks(a0, b0, step, pairs, one_sided=()):
        sums = {}

        def first(m, za, zb):
            kern[m] = matern(dot(left[a0 + za], right[b0 + zb], 1, 0))

        def add(key, value):
            sums[key] = value if key not in sums else sums[key] + value

        def second(m, za, zb):
            block = kern[m]
            a, b = a0 + za, b0 + zb
            slot = 13 + step + (zb - za)
            add(("a", za), dot(probe(b, a, slot), block, 1, 1))
            if (za, zb) not in one_sided:
                add(("b", zb), dot(probe(a, b, 26 - slot), block, 1, 0))

        late = 2
        for m in range(len(pairs) + late):
            if m < len(pairs):
                first(m, *pairs[m])
            if m >= late:
                second(m - late, *pairs[m - late])
        for (side, z), value in sums.items():
            at_box = (a0 if side == "a" else b0) + z
            acc[at_box] = acc[at_box] + value

    loop(BOXES, lambda i: prepare(i, True))

    def own_pair(i):
        d, j = i // 2 + 1, lax.rem(i, 2)
        a = j * (1 + 1 // d)
        b = a + d - 2 * a * (d // 3)
        x = lambda p: p // 2
        y = lambda p: 1 - lax.rem((p + 1) // 2, 2)
        blocks(4 * a, 4 * b, 9 * (x(b) - x(a)) + 3 * (y(b) - y(a)), Z_PAIRS)

    def tx_pair(i):
        xa, xb = lax.rem(i, 2), i // 2
        blocks(12 * xa, BOXES + 4 * xb, 9 * (xb - xa) + 3, Z_PAIRS)

    def ty_pair(i):
        ya, p = lax.rem(i, 2), i // 2
        blocks(8 + 4 * ya, BOXES + 8 + 4 * p, 9 + 3 * (1 - p - ya), Z_PAIRS)

    def corner_pair(i):
        blocks(12 - 4 * i, BOXES + 16 + 4 * i, 9 + 3 * (1 - 2 * i), Z_PAIRS)

    def column(i):
        same = tuple((z, z) for z in range(4))
        blocks(4 * i, 4 * i, 0, same + ((0, 1), (1, 2), (2, 3)), same)

    loop(6, own_pair)
    finish_round(0)
    send_round(1)
    for j in range(4):
        wait_recv(halo(j))
    loop(REMOTE, lambda i: prepare(BOXES + i, False))
    loop(4, tx_pair)
    reply(0).start()
    finish_round(1)
    send_round(2)
    loop(4, ty_pair)
    reply(1).start()
    loop(2, corner_pair)
    reply(2).start()
    reply(3).start()
    finish_round(2)
    loop(4, column)
    for i in range(5):
        gram_out[8 + i] = jnp.concatenate([grams[2 * i], grams[2 * i + 1]], axis=1)
    for j in range(4):
        wait_recv(reply(j))
    for i in range(BOXES):
        value = acc[i]
        for dy, dx, start, count, at_row in HALO:
            if start <= i < start + count:
                value = value + back[at_row + i - start]
        near_out[i] = value
    for j in range(4):
        wait_send(halo(j))
        wait_send(reply(j))
    for r in range(3):
        for q in range(1, 8):
            wait_send(exchange(r, q))


def factor_pairs(x, pairs):
    lane = lax.broadcasted_iota(jnp.int32, (8, 128), 1)
    sub = lax.broadcasted_iota(jnp.int32, (8, 128), 0)
    half = lane - lane % RANK
    spread = lambda v: jnp.broadcast_to(v, (8, 128))
    for j in range(0, RANK, 2):
        top = j // 8
        i0, i1 = half + j, half + j + 1
        pick = lambda v, idx: jnp.take_along_axis(v, idx, axis=1)
        for p in pairs:
            r0, r1 = spread(x[p, j : j + 1, :]), spread(x[p, j + 1 : j + 2, :])
            a, b, c = pick(r0, i0), pick(r0, i1), pick(r1, i1)
            sa = lax.rsqrt(a)
            out0 = r0 * sa
            inv = sa * sa
            t = b * inv
            sc = lax.rsqrt(c - b * t)
            out1 = (r1 - t * r0) * sc
            q1 = out1 * sc
            q0 = r0 * inv - t * q1
            for v in range(top, 8):
                old = x[p, 8 * v : 8 * v + 8, :]
                new = old - pick(old, i0) * q0 - pick(old, i1) * q1
                if v == top:
                    at = j - 8 * top
                    new = jnp.where(sub < at, old, jnp.where(sub == at, out0, jnp.where(sub == at + 1, out1, new)))
                x[p, 8 * v : 8 * v + 8, :] = new


def factor_kernel(near, gram, near_out, leaf_out, anc_out, x):
    for i, k in enumerate(BOX_AT):
        near_out[0, 0, :, k * PTS : (k + 1) * PTS] = near[i]
    x[...] = gram[...]
    factor_pairs(x, range(13))
    r = lax.broadcasted_iota(jnp.int32, (RANK, RANK), 0)
    c = lax.broadcasted_iota(jnp.int32, (RANK, RANK), 1)
    for p in range(13):
        for h in range(2):
            m = jnp.where(c >= r, x[p, :, RANK * h : RANK * (h + 1)], 0.0)
            if p < 8:
                leaf_out[0, 0, 2 * p + h] = m
            else:
                anc_out[0, 0, 2 * (p - 8) + h] = m


def vmem():
    return pl.BlockSpec(memory_space=pltpu.VMEM)


def on_device(sizes, comm, points, probes, near_boxes, leaf_bases, box_transfer, upper_transfer):
    near, gram = pl.pallas_call(
        functools.partial(main_kernel, sizes, comm),
        out_shape=(
            jax.ShapeDtypeStruct((BOXES, 8, PTS), F32),
            jax.ShapeDtypeStruct((13, RANK, 128), F32),
        ),
        in_specs=[vmem()] * 6,
        out_specs=(vmem(), vmem()),
        scratch_shapes=[
            pltpu.VMEM((BOXES + REMOTE, 16, PTS), F32),
            pltpu.VMEM((BOXES, PTS, 48), BF16),
            pltpu.VMEM((BOXES + REMOTE, 48, PTS), BF16),
            pltpu.VMEM((BOXES + REMOTE, 32, 128), F32),
            pltpu.VMEM((BOXES + REMOTE, 8, PTS), F32),
            pltpu.VMEM((REMOTE, 8, PTS), F32),
            pltpu.VMEM((10, PTS, PTS), BF16),
            pltpu.VMEM((10, RANK, RANK), F32),
            pltpu.VMEM((3, 3, 32, 128), F32),
            pltpu.VMEM((3, 7, 3, 32, 128), F32),
            pltpu.SemaphoreType.DMA((4,)),
            pltpu.SemaphoreType.DMA((4,)),
            pltpu.SemaphoreType.DMA((4,)),
            pltpu.SemaphoreType.DMA((4,)),
            pltpu.SemaphoreType.DMA((21,)),
            pltpu.SemaphoreType.DMA((21,)),
        ],
        compiler_params=pltpu.CompilerParams(
            collective_id=0 if comm else None, has_side_effects=True, vmem_limit_bytes=48 * 2**20
        ),
        name="near_and_grams",
    )(points, probes, near_boxes, leaf_bases, box_transfer, upper_transfer)
    return pl.pallas_call(
        factor_kernel,
        out_shape=(
            jax.ShapeDtypeStruct((1, 1, 8, BOXES * PTS), F32),
            jax.ShapeDtypeStruct((1, 1, BOXES, RANK, RANK), F32),
            jax.ShapeDtypeStruct((1, 1, 10, RANK, RANK), F32),
        ),
        in_specs=[vmem()] * 2,
        out_specs=(vmem(),) * 3,
        scratch_shapes=[pltpu.VMEM((13, RANK, 128), F32)],
        compiler_params=pltpu.CompilerParams(vmem_limit_bytes=32 * 2**20),
        name="factors",
    )(near, gram)


def solution(mesh):
    return jax.shard_map(
        functools.partial(on_device, (mesh.shape["ty"], mesh.shape["tx"]), True),
        mesh=mesh,
        in_specs=(
            P("ty", "tx", None, None),
            P("ty", "tx", None, None),
            P("ty", "tx", None, None),
            P("ty", "tx", None, None),
            P("ty", "tx", None, None, None),
            P(),
        ),
        out_specs=(
            P("ty", "tx", None, None),
            P("ty", "tx", None, None, None),
            P("ty", "tx", None, None, None),
        ),
        check_vma=False,
    )
```

```python
import functools
import math

import jax
import jax.numpy as jnp
from jax import lax
from jax.experimental import pallas as pl
from jax.experimental.pallas import tpu as pltpu
from jax.sharding import PartitionSpec as P

MESH = pl.DeviceIdType.MESH
HIGHEST = lax.Precision.HIGHEST
F32, BF16 = jnp.float32, jnp.bfloat16
LOG2E = 1.0 / math.log(2.0)
ALPHA = math.sqrt(3.0)
BOXES, PTS, RANK = 16, 256, 64
COLUMNS = ((0, 1), (0, 0), (1, 0), (1, 1))
BOX_AT = tuple(x + 2 * y + 4 * z for x, y in COLUMNS for z in range(4))
HALO = ((0, -1, 4, 8, 0), (-1, 0, 0, 8, 8), (-1, -1, 4, 4, 16), (-1, 1, 0, 4, 20))
REMOTE = 24
Z_PAIRS = tuple((a, b) for a in range(4) for b in range(4) if abs(a - b) <= 1)


def dot(a, b, ca, cb, precision=None):
    return lax.dot_general(
        a, b, (((ca,), (cb,)), ((), ())), precision=precision, preferred_element_type=F32
    )


def split3(value):
    high = value.astype(BF16).astype(F32)
    rest = value - high
    mid = rest.astype(BF16).astype(F32)
    return high, mid, (rest - mid).astype(BF16).astype(F32)


def features(rows, center, left):
    sub = lax.broadcasted_iota(jnp.int32, rows.shape, 0)
    cy, cx = center
    mid = jnp.where(sub == 0, cy, jnp.where(sub == 1, cx, 2.0))
    y = jnp.where(sub < 3, (rows - mid) * ALPHA, 0.0)
    norm = jnp.sum(y * y, axis=0, keepdims=True)
    zero = jnp.zeros_like(y)
    if left:
        h, m, l = split3(jnp.where(sub == 3, norm, y))
        one = jnp.where(sub == 4, 1.0, 0.0)
        coord = lambda v: jnp.where(sub < 3, -2.0 * v, 0.0)
        lead = lambda c, n: jnp.where(sub < 3, -2.0 * c, jnp.where(sub == 3, n, one))
        parts = (lead(h, h), lead(h, m), lead(m, l), coord(m), coord(h), coord(l))
    else:
        h, m, l = split3(jnp.where(sub == 4, norm, y))
        one = jnp.where(sub == 3, 1.0, 0.0)
        parts = (h + one, m + one, jnp.where(sub < 3, h, l) + one, m, l, h)
    return jnp.concatenate(parts, axis=0).astype(BF16)


def matern(square):
    s = jnp.maximum(square, 1e-12)
    c = s * lax.rsqrt(s)
    return ((1.0 + c) * jnp.exp2(c * -LOG2E)).astype(BF16)


def halves(packed):
    return jnp.concatenate([packed[:, :RANK], packed[:, RANK:]], axis=0)


def packed(full):
    return jnp.concatenate([full[:32], full[32:]], axis=1)


def remote(src, dst, send, recv, device, comm):
    if comm:
        return pltpu.make_async_remote_copy(
            src_ref=src, dst_ref=dst, send_sem=send, recv_sem=recv, device_id=device, device_id_type=MESH
        )
    return None


def main_kernel(sizes, comm, pts_in, prb_in, near_in, leaf_in, trans_in, upper_in,
                near_out, leaf_out, gram_out,
                pts, prb, near, leaf, trans, upper, loaded,
                box, left, right, mask, acc, back, kern, grams, paths, tree_out, tree_in,
                x0, x1, x2, x3, x4, x5, x6, x7,
                halo_send, halo_recv, back_send, back_recv, tree_send, tree_recv):
    xs = (x0, x1, x2, x3, x4, x5, x6, x7)
    loads = [
        pltpu.make_async_copy(src, dst, loaded.at[i])
        for i, (src, dst) in enumerate((
            (pts_in, pts), (prb_in.at[0, 0], prb), (near_in.at[0, 0], near),
            (leaf_in.at[0, 0], leaf), (trans_in.at[0, 0], trans), (upper_in, upper)))
    ]
    for load in loads:
        load.start()
    n_ty, n_tx = sizes
    ty, tx = (lax.axis_index("ty"), lax.axis_index("tx")) if comm else (jnp.int32(0), jnp.int32(0))
    center = ((2 * ty + 1).astype(F32), (2 * tx + 1).astype(F32))

    def at(dy, dx):
        return (lax.rem(ty + dy + n_ty, n_ty), lax.rem(tx + dx + n_tx, n_tx))

    bits = [lax.rem(tx // 2**i, 2) for i in range(5)] + [lax.rem(ty // 2**i, 2) for i in range(4)]

    def relative(level, q):
        row, col = ty, tx
        for i in range(3):
            if q >> i & 1:
                b = level + i
                if b < 5:
                    col = col + 2**b * (1 - 2 * bits[b])
                else:
                    row = row + 2 ** (b - 5) * (1 - 2 * bits[b])
        return (row, col)

    peers = [at(*h[:2]) for h in HALO] + [at(-h[0], -h[1]) for h in HALO]
    peers += [relative(3 * r, q) for r in range(3) for q in range(1, 8)]
    if comm:
        barrier = pltpu.get_barrier_semaphore()
        for peer in peers:
            pl.semaphore_signal(barrier, inc=1, device_id=peer, device_id_type=MESH)

    for load in loads[:3]:
        load.wait()
    for i, k in enumerate(BOX_AT):
        cols = slice(k * PTS, (k + 1) * PTS)
        for c in range(3):
            for h in range(2):
                box[i, c : c + 1, 128 * h : 128 * h + 128] = pts[c, 2 * k + h : 2 * k + h + 1, :]
        box[i, 8:16, :] = prb[:, cols]
        box[i, 3:8, :] = jnp.zeros((5, PTS), F32)
        box[i, 3:4, 0:27] = jnp.where(near[k : k + 1, :] >= 0, 1.0, 0.0)

    if comm:
        pl.semaphore_wait(barrier, len(peers))

    def halo(j):
        dy, dx, first, count, row = HALO[j]
        src, dst = box.at[pl.ds(first, count)], box.at[pl.ds(BOXES + row, count)]
        if comm:
            return pltpu.make_async_remote_copy(
                src_ref=src, dst_ref=dst, send_sem=halo_send.at[j], recv_sem=halo_recv.at[j],
                device_id=at(dy, dx), device_id_type=MESH)
        return pltpu.make_async_copy(src, dst, halo_recv.at[j])

    def reply(j):
        dy, dx, first, count, row = HALO[j]
        src, dst = acc.at[pl.ds(BOXES + row, count)], back.at[pl.ds(row, count)]
        if comm:
            return pltpu.make_async_remote_copy(
                src_ref=src, dst_ref=dst, send_sem=back_send.at[j], recv_sem=back_recv.at[j],
                device_id=at(-dy, -dx), device_id_type=MESH)
        return pltpu.make_async_copy(src, dst, back_recv.at[j])

    def exchange(r, q):
        count = 3 if q == 1 else 2 if q < 4 else 1
        src, dst = tree_out.at[r, pl.ds(0, count)], tree_in.at[r, q - 1, pl.ds(0, count)]
        j = 7 * r + q - 1
        if comm:
            return pltpu.make_async_remote_copy(
                src_ref=src, dst_ref=dst, send_sem=tree_send.at[j], recv_sem=tree_recv.at[j],
                device_id=relative(3 * r, q), device_id_type=MESH)
        return pltpu.make_async_copy(src, dst, tree_recv.at[j])

    def wait_send(copy):
        if comm:
            copy.wait_send()

    def wait_recv(copy):
        if comm:
            copy.wait_recv()
        else:
            copy.wait()

    for j in range(4):
        halo(j).start()

    for load in loads[3:]:
        load.wait()
    for r in range(3):
        path = None
        for i in range(3):
            step = upper[3 * r + i, bits[3 * r + i]]
            path = step if path is None else dot(path, step, 1, 0, HIGHEST)
            paths[3 * r + i] = path
    total = jnp.zeros((RANK, RANK), F32)
    pair = []
    for k in range(BOXES):
        v = leaf[:, k * PTS : (k + 1) * PTS]
        stack = jnp.concatenate(split3(v), axis=0).astype(BF16)
        c = dot(stack, stack, 1, 1)
        g = c[128:, :64] + c[:64, 128:] + c[64:128, 64:128]
        g = g + (c[:64, 64:128] + c[64:128, :64]) + c[:64, :64]
        pair.append(g)
        if k % 2:
            xs[k // 2][...] = jnp.concatenate(pair, axis=1)
            pair = []
        t = trans[k]
        total = total + dot(t, dot(g, t, 1, 0, HIGHEST), 0, 0, HIGHEST)
    grams[0] = total

    def send_round(r):
        node = grams[3 * r]
        for i in range(3):
            path = paths[3 * r + i]
            term = dot(path, dot(node, path, 1, 0, HIGHEST), 0, 0, HIGHEST)
            tree_out[r, 2 - i] = packed(term)
        for q in range(1, 8):
            exchange(r, q).start()

    def finish_round(r):
        for q in range(1, 8):
            wait_recv(exchange(r, q))
        for i in range(3):
            node = tree_out[r, 2 - i]
            for q in range(1, 2 ** (i + 1)):
                node = node + tree_in[r, q - 1, 2 - i]
            grams[3 * r + i + 1] = halves(node)

    send_round(0)

    lane = lax.broadcasted_iota(jnp.int32, (32, 128), 1)
    row = lax.broadcasted_iota(jnp.int32, (32, 128), 0)
    ones = jnp.ones((128, 128), BF16)
    diag = lax.broadcasted_iota(jnp.int32, (PTS, PTS), 0) == lax.broadcasted_iota(jnp.int32, (PTS, PTS), 1)
    eye = jnp.where(diag, 1.0, 0.0).astype(BF16)

    def prepare(i, own):
        rows = box[i, 0:8, :]
        right[i] = features(rows, center, False)
        if own:
            left[i] = dot(eye, features(rows, center, True), 1, 1).astype(BF16)
        slots = jnp.where(lane == row, box[i, 3:4, 0:128], 0.0).astype(BF16)
        mask[i] = dot(slots, ones, 1, 0)
        acc[i] = jnp.zeros((8, PTS), F32)

    def loop(n, body, unroll=2):
        lax.fori_loop(0, n, lambda i, c: (body(i), c)[1], 0, unroll=unroll)

    def probe(i, owner, slot):
        m = mask[owner, pl.ds(slot, 1), :]
        return (box[i, 8:16, :] * jnp.concatenate([m, m], axis=1)).astype(BF16)

    def factor(t):
        for p in range(8):
            factor_step(xs[p], leaf_out, p, 2 * t)

    def blocks(a0, b0, step, pairs, one_sided=(), steps=(), base=0):
        sums = {}

        def first(m, za, zb):
            kern[base + m] = matern(dot(left[a0 + za], right[b0 + zb], 1, 0))

        def add(key, value):
            sums[key] = value if key not in sums else sums[key] + value

        def second(m, za, zb):
            block = kern[base + m]
            a, b = a0 + za, b0 + zb
            slot = 13 + step + (zb - za)
            add(("a", za), dot(probe(b, a, slot), block, 1, 1))
            if (za, zb) not in one_sided:
                add(("b", zb), dot(probe(a, b, 26 - slot), block, 1, 0))

        late = 2
        for m in range(len(pairs) + late):
            if m % 5 == 1 and m // 5 < len(steps):
                factor(steps[m // 5])
            if m < len(pairs):
                first(m, *pairs[m])
            if m >= late:
                second(m - late, *pairs[m - late])
        for (side, z), value in sums.items():
            at_box = (a0 if side == "a" else b0) + z
            acc[at_box] = acc[at_box] + value

    loop(BOXES, lambda i: prepare(i, True), 4)

    def own_pair(i, base=0):
        d, j = i // 2 + 1, lax.rem(i, 2)
        a = j * (1 + 1 // d)
        b = a + d - 2 * a * (d // 3)
        x = lambda p: p // 2
        y = lambda p: 1 - lax.rem((p + 1) // 2, 2)
        blocks(4 * a, 4 * b, 9 * (x(b) - x(a)) + 3 * (y(b) - y(a)), Z_PAIRS, base=base, steps=(0 + 2 * i, 1 + 2 * i))

    def tx_pair(i, base=0):
        xa, xb = lax.rem(i, 2), i // 2
        blocks(12 * xa, BOXES + 4 * xb, 9 * (xb - xa) + 3, Z_PAIRS, base=base, steps=(12 + 2 * i, 13 + 2 * i))

    def ty_pair(i, base=0):
        ya, p = lax.rem(i, 2), i // 2
        blocks(8 + 4 * ya, BOXES + 8 + 4 * p, 9 + 3 * (1 - p - ya), Z_PAIRS, base=base, steps=(20 + 2 * i, 21 + 2 * i))

    def corner_pair(i, base=0):
        blocks(12 - 4 * i, BOXES + 16 + 4 * i, 9 + 3 * (1 - 2 * i), Z_PAIRS, base=base, steps=(28 + 2 * i, 29 + 2 * i))

    def column(i, base=0):
        same = tuple((z, z) for z in range(4))
        blocks(4 * i, 4 * i, 0, same + ((0, 1), (1, 2), (2, 3)), same, base=base)

    loop(3, lambda i: (own_pair(2 * i), own_pair(2 * i + 1, 10)), 1)
    finish_round(0)
    send_round(1)
    for j in range(4):
        wait_recv(halo(j))
    loop(REMOTE, lambda i: prepare(BOXES + i, False), 4)
    loop(2, lambda i: (tx_pair(2 * i), tx_pair(2 * i + 1, 10)), 1)
    reply(0).start()
    finish_round(1)
    send_round(2)
    loop(2, lambda i: (ty_pair(2 * i), ty_pair(2 * i + 1, 10)), 1)
    reply(1).start()
    loop(1, lambda i: (corner_pair(2 * i), corner_pair(2 * i + 1, 10)), 1)
    reply(2).start()
    reply(3).start()
    finish_round(2)
    loop(2, lambda i: (column(2 * i), column(2 * i + 1, 10)), 1)
    for i in range(5):
        gram_out[i] = jnp.concatenate([grams[2 * i], grams[2 * i + 1]], axis=1)
    for j in range(4):
        wait_recv(reply(j))
    for i in range(BOXES):
        value = acc[i]
        for dy, dx, start, count, at_row in HALO:
            if start <= i < start + count:
                value = value + back[at_row + i - start]
        near_out[i] = value
    for j in range(4):
        wait_send(halo(j))
        wait_send(reply(j))
    for r in range(3):
        for q in range(1, 8):
            wait_send(exchange(r, q))


def factor_step(x, out, p, j, top=0):
    lane = lax.broadcasted_iota(jnp.int32, (8, 128), 1)
    half = lane - lane % RANK
    i0, i1 = half + j, half + j + 1
    pick = lambda v, idx: jnp.take_along_axis(v, idx, axis=1)
    r0 = jnp.broadcast_to(x[pl.ds(j, 1), :], (8, 128))
    r1 = jnp.broadcast_to(x[pl.ds(j + 1, 1), :], (8, 128))
    a, b, c = pick(r0, i0), pick(r0, i1), pick(r1, i1)
    sa = lax.rsqrt(a)
    inv = sa * sa
    t = b * inv
    sc = lax.rsqrt(c - b * t)
    out0, out1 = r0 * sa, (r1 - t * r0) * sc
    out[p, pl.ds(j, 1), :] = out0[0:1]
    out[p, pl.ds(j + 1, 1), :] = out1[0:1]
    q1 = out1 * sc
    q0 = r0 * inv - t * q1
    for v in range(top, 8):
        rows = slice(8 * v, 8 * v + 8)
        old = x[rows, :]
        x[rows, :] = old - pick(old, i0) * q0 - pick(old, i1) * q1


def factor_kernel(near, leaf_in, gram_in, near_out, leaf_out, anc_out, leaf, gram, done, x0, x1, x2, x3, x4, sems):
    xs = (x0, x1, x2, x3, x4)
    copies = [pltpu.make_async_copy(gram_in, gram, sems.at[16]), pltpu.make_async_copy(leaf_in, leaf, sems.at[17])]
    for i, k in enumerate(BOX_AT):
        cols = pl.ds(k * PTS, PTS)
        copies.append(pltpu.make_async_copy(near.at[i], near_out.at[0, 0, :, cols], sems.at[i]))
    for copy in copies:
        copy.start()
    copies[0].wait()
    for p, x in enumerate(xs):
        x[...] = gram[p]
    r = lax.broadcasted_iota(jnp.int32, (RANK, RANK), 0)
    c = lax.broadcasted_iota(jnp.int32, (RANK, RANK), 1)
    triangle = lambda m, h: jnp.where(c >= r, m[:, RANK * h : RANK * (h + 1)], 0.0)
    copies[1].wait()
    for p in range(8):
        for h in range(2):
            leaf_out[0, 0, 2 * p + h] = triangle(leaf[p], h)
    for j in range(0, RANK, 2):
        for p, x in enumerate(xs):
            factor_step(x, done, p, j, j // 8)
    for p in range(5):
        for h in range(2):
            anc_out[0, 0, 2 * p + h] = triangle(done[p], h)
    for copy in copies[2:]:
        copy.wait()


def vmem():
    return pl.BlockSpec(memory_space=pltpu.VMEM)


def on_device(sizes, comm, points, probes, near_boxes, leaf_bases, box_transfer, upper_transfer):
    near, leaf, gram = pl.pallas_call(
        functools.partial(main_kernel, sizes, comm),
        out_shape=(
            jax.ShapeDtypeStruct((BOXES, 8, PTS), F32),
            jax.ShapeDtypeStruct((8, RANK, 128), F32),
            jax.ShapeDtypeStruct((5, RANK, 128), F32),
        ),
        in_specs=[pl.BlockSpec(memory_space=pl.ANY)] * 6,
        out_specs=(vmem(),) * 3,
        scratch_shapes=[
            pltpu.VMEM((3, 32, 128), F32),
            pltpu.VMEM((8, BOXES * PTS), F32),
            pltpu.VMEM((BOXES, 27), jnp.int32),
            pltpu.VMEM((RANK, BOXES * PTS), F32),
            pltpu.VMEM((BOXES, RANK, RANK), F32),
            pltpu.VMEM((9, 2, RANK, RANK), F32),
            pltpu.SemaphoreType.DMA((6,)),
            pltpu.VMEM((BOXES + REMOTE, 16, PTS), F32),
            pltpu.VMEM((BOXES, PTS, 48), BF16),
            pltpu.VMEM((BOXES + REMOTE, 48, PTS), BF16),
            pltpu.VMEM((BOXES + REMOTE, 32, 128), F32),
            pltpu.VMEM((BOXES + REMOTE, 8, PTS), F32),
            pltpu.VMEM((REMOTE, 8, PTS), F32),
            pltpu.VMEM((20, PTS, PTS), BF16),
            pltpu.VMEM((10, RANK, RANK), F32),
            pltpu.VMEM((9, RANK, RANK), F32),
            pltpu.VMEM((3, 3, 32, 128), F32),
            pltpu.VMEM((3, 7, 3, 32, 128), F32),
            *[pltpu.VMEM((RANK, 128), F32)] * 8,
            pltpu.SemaphoreType.DMA((4,)),
            pltpu.SemaphoreType.DMA((4,)),
            pltpu.SemaphoreType.DMA((4,)),
            pltpu.SemaphoreType.DMA((4,)),
            pltpu.SemaphoreType.DMA((21,)),
            pltpu.SemaphoreType.DMA((21,)),
        ],
        compiler_params=pltpu.CompilerParams(
            collective_id=0 if comm else None, has_side_effects=True, vmem_limit_bytes=62 * 2**20
        ),
        name="near_and_grams",
    )(points.reshape(3, 32, 128), probes, near_boxes, leaf_bases, box_transfer, upper_transfer)
    return pl.pallas_call(
        factor_kernel,
        out_shape=(
            jax.ShapeDtypeStruct((1, 1, 8, BOXES * PTS), F32),
            jax.ShapeDtypeStruct((1, 1, BOXES, RANK, RANK), F32),
            jax.ShapeDtypeStruct((1, 1, 10, RANK, RANK), F32),
        ),
        in_specs=[pl.BlockSpec(memory_space=pl.ANY)] * 3,
        out_specs=(pl.BlockSpec(memory_space=pl.ANY), vmem(), vmem()),
        scratch_shapes=[
            pltpu.VMEM((8, RANK, 128), F32),
            pltpu.VMEM((5, RANK, 128), F32),
            pltpu.VMEM((5, RANK, 128), F32),
            *[pltpu.VMEM((RANK, 128), F32)] * 5,
            pltpu.SemaphoreType.DMA((18,)),
        ],
        compiler_params=pltpu.CompilerParams(vmem_limit_bytes=62 * 2**20),
        name="factors",
    )(near, leaf, gram)


def solution(mesh):
    return jax.shard_map(
        functools.partial(on_device, (mesh.shape["ty"], mesh.shape["tx"]), True),
        mesh=mesh,
        in_specs=(
            P("ty", "tx", None, None),
            P("ty", "tx", None, None),
            P("ty", "tx", None, None),
            P("ty", "tx", None, None),
            P("ty", "tx", None, None, None),
            P(),
        ),
        out_specs=(
            P("ty", "tx", None, None),
            P("ty", "tx", None, None, None),
            P("ty", "tx", None, None, None),
        ),
        check_vma=False,
    )
```

```python
import functools
import math

import jax
import jax.numpy as jnp
from jax import lax
from jax.experimental import pallas as pl
from jax.experimental.pallas import tpu as pltpu
from jax.sharding import PartitionSpec as P

MESH = pl.DeviceIdType.MESH
HIGHEST = lax.Precision.HIGHEST
F32, BF16 = jnp.float32, jnp.bfloat16
LOG2E = 1.0 / math.log(2.0)
ALPHA = math.sqrt(3.0)
BOXES, PTS, RANK = 16, 256, 64
TEST_TY = 6
COLUMNS = ((0, 1), (0, 0), (1, 0), (1, 1))
BOX_AT = tuple(x + 2 * y + 4 * z for x, y in COLUMNS for z in range(4))
HALO = ((0, -1, 4, 8, 0), (-1, 0, 0, 8, 8), (-1, -1, 4, 4, 16), (-1, 1, 0, 4, 20))
REMOTE = 24
Z_PAIRS = tuple((a, b) for a in range(4) for b in range(4) if abs(a - b) <= 1)


def dot(a, b, ca, cb, precision=None):
    return lax.dot_general(
        a, b, (((ca,), (cb,)), ((), ())), precision=precision, preferred_element_type=F32
    )


def split3(value):
    high = value.astype(BF16).astype(F32)
    rest = value - high
    mid = rest.astype(BF16).astype(F32)
    return high, mid, (rest - mid).astype(BF16).astype(F32)


def features(rows, center, left):
    sub = lax.broadcasted_iota(jnp.int32, rows.shape, 0)
    cy, cx = center
    mid = jnp.where(sub == 0, cy, jnp.where(sub == 1, cx, 2.0))
    y = jnp.where(sub < 3, (rows - mid) * ALPHA, 0.0)
    norm = jnp.sum(y * y, axis=0, keepdims=True)
    zero = jnp.zeros_like(y)
    if left:
        h, m, l = split3(jnp.where(sub == 3, norm, y))
        one = jnp.where(sub == 4, 1.0, 0.0)
        coord = lambda v: jnp.where(sub < 3, -2.0 * v, 0.0)
        lead = lambda c, n: jnp.where(sub < 3, -2.0 * c, jnp.where(sub == 3, n, one))
        parts = (lead(h, h), lead(h, m), lead(m, l), coord(m), coord(h), coord(l))
    else:
        h, m, l = split3(jnp.where(sub == 4, norm, y))
        one = jnp.where(sub == 3, 1.0, 0.0)
        parts = (h + one, m + one, jnp.where(sub < 3, h, l) + one, m, l, h)
    return jnp.concatenate(parts, axis=0).astype(BF16)


def matern(square):
    s = jnp.maximum(square, 1e-12)
    c = s * lax.rsqrt(s)
    return ((1.0 + c) * jnp.exp2(c * -LOG2E)).astype(BF16)


def halves(packed):
    return jnp.concatenate([packed[:, :RANK], packed[:, RANK:]], axis=0)


def packed(full):
    return jnp.concatenate([full[:32], full[32:]], axis=1)


def remote(src, dst, send, recv, device, comm):
    if comm:
        return pltpu.make_async_remote_copy(
            src_ref=src, dst_ref=dst, send_sem=send, recv_sem=recv, device_id=device, device_id_type=MESH
        )
    return None


def main_kernel(sizes, comm, pts_in, prb_in, near_in, leaf_in, trans_in, upper_in,
                near_out, leaf_out, gram_out,
                pts, prb, near, leaf, trans, upper, loaded,
                box, left, right, mask, acc, back, kern, grams, paths, tree_out, tree_in,
                x0, x1, x2, x3, x4, x5, x6, x7,
                halo_send, halo_recv, back_send, back_recv, tree_send, tree_recv):
    xs = (x0, x1, x2, x3, x4, x5, x6, x7)
    loads = [
        pltpu.make_async_copy(src, dst, loaded.at[i])
        for i, (src, dst) in enumerate((
            (pts_in, pts), (prb_in.at[0, 0], prb), (near_in.at[0, 0], near),
            (leaf_in.at[0, 0], leaf), (trans_in.at[0, 0], trans), (upper_in, upper)))
    ]
    for load in loads:
        load.start()
    n_ty, n_tx = sizes
    ty, tx = (lax.axis_index("ty"), lax.axis_index("tx")) if comm else (jnp.int32(TEST_TY), jnp.int32(0))
    center = ((2 * ty + 1).astype(F32), (2 * tx + 1).astype(F32))

    def at(dy, dx):
        return (lax.rem(ty + dy + n_ty, n_ty), lax.rem(tx + dx + n_tx, n_tx))

    bits = [lax.rem(tx // 2**i, 2) for i in range(5)] + [lax.rem(ty // 2**i, 2) for i in range(4)]

    def relative(level, q):
        row, col = ty, tx
        for i in range(3):
            if q >> i & 1:
                b = level + i
                if b < 5:
                    col = col + 2**b * (1 - 2 * bits[b])
                else:
                    row = row + 2 ** (b - 5) * (1 - 2 * bits[b])
        return (row, col)

    peers = [at(*h[:2]) for h in HALO] + [at(-h[0], -h[1]) for h in HALO]
    peers += [relative(3 * r, q) for r in range(3) for q in range(1, 8)]
    if comm:
        barrier = pltpu.get_barrier_semaphore()
        for peer in peers:
            pl.semaphore_signal(barrier, inc=1, device_id=peer, device_id_type=MESH)

    z = ty // 2 + 3 * (1 - (ty * n_tx + tx + n_ty * n_tx - 1) // (n_ty * n_tx))
    near_z, first_z = 1 - z // 4, 1 - (z + 7) // 8
    pairs_ahead = near_z * (4 - z) - first_z
    columns_ahead = near_z + first_z
    columns_next = columns_ahead + 1 - near_z

    @pl.when(ty == n_ty - 1)
    def _():
        box[24:40] = jnp.zeros((16, 16, PTS), F32)

    @pl.when(ty == 0)
    def _():
        back[8:24] = jnp.zeros((16, 8, PTS), F32)

    for load in loads[:3]:
        load.wait()
    for i, k in enumerate(BOX_AT):
        cols = slice(k * PTS, (k + 1) * PTS)
        for c in range(3):
            for h in range(2):
                box[i, c : c + 1, 128 * h : 128 * h + 128] = pts[c, 2 * k + h : 2 * k + h + 1, :]
        box[i, 8:16, :] = prb[:, cols]
        box[i, 3:8, :] = jnp.zeros((5, PTS), F32)
        box[i, 3:4, 0:27] = jnp.where(near[k : k + 1, :] >= 0, 1.0, 0.0)

    def halo(j):
        dy, dx, first, count, row = HALO[j]
        src, dst = box.at[pl.ds(first, count)], box.at[pl.ds(BOXES + row, count)]
        if comm:
            return pltpu.make_async_remote_copy(
                src_ref=src, dst_ref=dst, send_sem=halo_send.at[j], recv_sem=halo_recv.at[j],
                device_id=at(dy, dx), device_id_type=MESH)
        return pltpu.make_async_copy(src, dst, halo_recv.at[j])

    def reply(j):
        dy, dx, first, count, row = HALO[j]
        src, dst = acc.at[pl.ds(BOXES + row, count)], back.at[pl.ds(row, count)]
        if comm:
            return pltpu.make_async_remote_copy(
                src_ref=src, dst_ref=dst, send_sem=back_send.at[j], recv_sem=back_recv.at[j],
                device_id=at(-dy, -dx), device_id_type=MESH)
        return pltpu.make_async_copy(src, dst, back_recv.at[j])

    def exchange(r, q):
        count = 3 if q == 1 else 2 if q < 4 else 1
        src, dst = tree_out.at[r, pl.ds(0, count)], tree_in.at[r, q - 1, pl.ds(0, count)]
        j = 7 * r + q - 1
        if comm:
            return pltpu.make_async_remote_copy(
                src_ref=src, dst_ref=dst, send_sem=tree_send.at[j], recv_sem=tree_recv.at[j],
                device_id=relative(3 * r, q), device_id_type=MESH)
        return pltpu.make_async_copy(src, dst, tree_recv.at[j])

    def wait_send(copy):
        if comm:
            copy.wait_send()

    def wait_recv(copy):
        if comm:
            copy.wait_recv()
        else:
            copy.wait()

    for load in loads[3:]:
        load.wait()
    for r in range(3):
        path = None
        for i in range(3):
            step = upper[3 * r + i, bits[3 * r + i]]
            path = step if path is None else dot(path, step, 1, 0, HIGHEST)
            paths[3 * r + i] = path
    total = jnp.zeros((RANK, RANK), F32)
    pair = []
    for k in range(BOXES):
        v = leaf[:, k * PTS : (k + 1) * PTS]
        stack = jnp.concatenate(split3(v), axis=0).astype(BF16)
        c = dot(stack, stack, 1, 1)
        g = c[128:, :64] + c[:64, 128:] + c[64:128, 64:128]
        g = g + (c[:64, 64:128] + c[64:128, :64]) + c[:64, :64]
        pair.append(g)
        if k % 2:
            xs[k // 2][...] = jnp.concatenate(pair, axis=1)
            pair = []
        t = trans[k]
        total = total + dot(t, dot(g, t, 1, 0, HIGHEST), 0, 0, HIGHEST)
    grams[0] = total

    def send_round(r):
        node = grams[3 * r]
        for i in range(3):
            path = paths[3 * r + i]
            term = dot(path, dot(node, path, 1, 0, HIGHEST), 0, 0, HIGHEST)
            tree_out[r, 2 - i] = packed(term)
        for q in range(1, 8):
            exchange(r, q).start()

    def finish_round(r):
        for q in range(1, 8):
            wait_recv(exchange(r, q))
        for i in range(3):
            node = tree_out[r, 2 - i]
            for q in range(1, 2 ** (i + 1)):
                node = node + tree_in[r, q - 1, 2 - i]
            grams[3 * r + i + 1] = halves(node)

    lane = lax.broadcasted_iota(jnp.int32, (32, 128), 1)
    row = lax.broadcasted_iota(jnp.int32, (32, 128), 0)
    ones = jnp.ones((128, 128), BF16)
    diag = lax.broadcasted_iota(jnp.int32, (PTS, PTS), 0) == lax.broadcasted_iota(jnp.int32, (PTS, PTS), 1)
    eye = jnp.where(diag, 1.0, 0.0).astype(BF16)

    def prepare(i, own):
        rows = box[i, 0:8, :]
        right[i] = features(rows, center, False)
        if own:
            left[i] = dot(eye, features(rows, center, True), 1, 1).astype(BF16)
        slots = jnp.where(lane == row, box[i, 3:4, 0:128], 0.0).astype(BF16)
        mask[i] = dot(slots, ones, 1, 0)
        acc[i] = jnp.zeros((8, PTS), F32)

    def loop(n, body, unroll=1, first=0):
        lax.fori_loop(first, n, lambda i, c: (body(i), c)[1], 0, unroll=unroll)

    def probe(i, owner, slot):
        m = mask[owner, pl.ds(slot, 1), :]
        return (box[i, 8:16, :] * jnp.concatenate([m, m], axis=1)).astype(BF16)

    def factor(t):
        for p in range(8):
            factor_step(xs[p], leaf_out, p, 2 * t)

    def blocks(a0, b0, step, pairs, one_sided=(), steps=(), base=0):
        sums = {}

        def first(m, za, zb):
            kern[base + m] = matern(dot(left[a0 + za], right[b0 + zb], 1, 0))

        def add(key, value):
            sums[key] = value if key not in sums else sums[key] + value

        def second(m, za, zb):
            block = kern[base + m]
            a, b = a0 + za, b0 + zb
            slot = 13 + step + (zb - za)
            add(("a", za), dot(probe(b, a, slot), block, 1, 1))
            if (za, zb) not in one_sided:
                add(("b", zb), dot(probe(a, b, 26 - slot), block, 1, 0))

        late = 2
        for m in range(len(pairs) + late):
            if m % 5 == 1 and m // 5 < len(steps):
                factor(steps[m // 5])
            if m < len(pairs):
                first(m, *pairs[m])
            if m >= late:
                second(m - late, *pairs[m - late])
        for (side, z), value in sums.items():
            at_box = (a0 if side == "a" else b0) + z
            acc[at_box] = acc[at_box] + value

    loop(BOXES, lambda i: prepare(i, True), 4)

    def own_pair(i, base, begin):
        d, j = i // 2 + 1, lax.rem(i, 2)
        a = j * (1 + 1 // d)
        b = a + d - 2 * a * (d // 3)
        x = lambda p: p // 2
        y = lambda p: 1 - lax.rem((p + 1) // 2, 2)
        blocks(4 * a, 4 * b, 9 * (x(b) - x(a)) + 3 * (y(b) - y(a)), Z_PAIRS, base=base, steps=(begin + 2 * i, begin + 1 + 2 * i))

    def tx_pair(i, base=0):
        xa, xb = lax.rem(i, 2), i // 2
        blocks(12 * xa, BOXES + 4 * xb, 9 * (xb - xa) + 3, Z_PAIRS, base=base, steps=(done + 0 + 2 * i, done + 1 + 2 * i))

    def ty_pair(i, base=0):
        ya, p = lax.rem(i, 2), i // 2
        blocks(8 + 4 * ya, BOXES + 8 + 4 * p, 9 + 3 * (1 - p - ya), Z_PAIRS, base=base, steps=(done + 8 + 2 * i, done + 9 + 2 * i))

    def corner_pair(i, base=0):
        blocks(12 - 4 * i, BOXES + 16 + 4 * i, 9 + 3 * (1 - 2 * i), Z_PAIRS, base=base, steps=(done + 16 + 2 * i, done + 17 + 2 * i))

    def column(i, base=0):
        same = tuple((z, z) for z in range(4))
        blocks(4 * i, 4 * i, 0, same + ((0, 1), (1, 2), (2, 3)), same, base=base)

    def own_pairs(first, last, begin):
        loop(last, lambda i: (own_pair(2 * i, 0, begin), own_pair(2 * i + 1, 10, begin)), 1, first)

    def columns(first, last):
        loop(last, lambda i: (column(2 * i), column(2 * i + 1, 10)), 1, first)

    own_pairs(0, pairs_ahead, 0)
    columns(0, columns_ahead)
    if comm:
        pl.semaphore_wait(barrier, len(peers))
    halo(0).start()

    @pl.when(ty > 0)
    def _():
        for j in range(1, 4):
            halo(j).start()

    send_round(0)
    columns(columns_ahead, columns_next)
    finish_round(0)
    send_round(1)
    columns(columns_next, 2)
    finish_round(1)
    send_round(2)
    wait_recv(halo(0))

    @pl.when(ty < n_ty - 1)
    def _():
        for j in range(1, 4):
            wait_recv(halo(j))

    loop(REMOTE, lambda i: prepare(BOXES + i, False), 4)
    done = 4 * pairs_ahead
    loop(2, lambda i: (tx_pair(2 * i), tx_pair(2 * i + 1, 10)))
    reply(0).start()
    loop(2, lambda i: (ty_pair(2 * i), ty_pair(2 * i + 1, 10)))
    loop(1, lambda i: (corner_pair(2 * i), corner_pair(2 * i + 1, 10)))

    @pl.when(ty < n_ty - 1)
    def _():
        for j in range(1, 4):
            reply(j).start()

    own_pairs(pairs_ahead, 3, 20)
    finish_round(2)
    for i in range(5):
        gram_out[i] = jnp.concatenate([grams[2 * i], grams[2 * i + 1]], axis=1)
    wait_recv(reply(0))

    @pl.when(ty > 0)
    def _():
        for j in range(1, 4):
            wait_recv(reply(j))

    for i in range(BOXES):
        value = acc[i]
        for dy, dx, start, count, at_row in HALO:
            if start <= i < start + count:
                value = value + back[at_row + i - start]
        near_out[i] = value
    wait_send(halo(0))
    wait_send(reply(0))

    @pl.when(ty > 0)
    def _():
        for j in range(1, 4):
            wait_send(halo(j))

    @pl.when(ty < n_ty - 1)
    def _():
        for j in range(1, 4):
            wait_send(reply(j))

    for r in range(3):
        for q in range(1, 8):
            wait_send(exchange(r, q))


def factor_step(x, out, p, j, top=0):
    lane = lax.broadcasted_iota(jnp.int32, (8, 128), 1)
    half = lane - lane % RANK
    i0, i1 = half + j, half + j + 1
    pick = lambda v, idx: jnp.take_along_axis(v, idx, axis=1)
    r0 = jnp.broadcast_to(x[pl.ds(j, 1), :], (8, 128))
    r1 = jnp.broadcast_to(x[pl.ds(j + 1, 1), :], (8, 128))
    a, b, c = pick(r0, i0), pick(r0, i1), pick(r1, i1)
    sa = lax.rsqrt(a)
    inv = sa * sa
    t = b * inv
    sc = lax.rsqrt(c - b * t)
    out0, out1 = r0 * sa, (r1 - t * r0) * sc
    out[p, pl.ds(j, 1), :] = out0[0:1]
    out[p, pl.ds(j + 1, 1), :] = out1[0:1]
    q1 = out1 * sc
    q0 = r0 * inv - t * q1
    for v in range(top, 8):
        rows = slice(8 * v, 8 * v + 8)
        old = x[rows, :]
        x[rows, :] = old - pick(old, i0) * q0 - pick(old, i1) * q1


def factor_kernel(near, leaf_in, gram_in, near_out, leaf_out, anc_out, leaf, gram, done, x0, x1, x2, x3, x4, sems):
    xs = (x0, x1, x2, x3, x4)
    copies = [pltpu.make_async_copy(gram_in, gram, sems.at[16]), pltpu.make_async_copy(leaf_in, leaf, sems.at[17])]
    for i, k in enumerate(BOX_AT):
        cols = pl.ds(k * PTS, PTS)
        copies.append(pltpu.make_async_copy(near.at[i], near_out.at[0, 0, :, cols], sems.at[i]))
    for copy in copies:
        copy.start()
    copies[0].wait()
    for p, x in enumerate(xs):
        x[...] = gram[p]
    r = lax.broadcasted_iota(jnp.int32, (RANK, RANK), 0)
    c = lax.broadcasted_iota(jnp.int32, (RANK, RANK), 1)
    triangle = lambda m, h: jnp.where(c >= r, m[:, RANK * h : RANK * (h + 1)], 0.0)
    copies[1].wait()
    for p in range(8):
        for h in range(2):
            leaf_out[0, 0, 2 * p + h] = triangle(leaf[p], h)
    for j in range(0, RANK, 2):
        for p, x in enumerate(xs):
            factor_step(x, done, p, j, j // 8)
    for p in range(5):
        for h in range(2):
            anc_out[0, 0, 2 * p + h] = triangle(done[p], h)
    for copy in copies[2:]:
        copy.wait()


def vmem():
    return pl.BlockSpec(memory_space=pltpu.VMEM)


def on_device(sizes, comm, points, probes, near_boxes, leaf_bases, box_transfer, upper_transfer):
    near, leaf, gram = pl.pallas_call(
        functools.partial(main_kernel, sizes, comm),
        out_shape=(
            jax.ShapeDtypeStruct((BOXES, 8, PTS), F32),
            jax.ShapeDtypeStruct((8, RANK, 128), F32),
            jax.ShapeDtypeStruct((5, RANK, 128), F32),
        ),
        in_specs=[pl.BlockSpec(memory_space=pl.ANY)] * 6,
        out_specs=(vmem(),) * 3,
        scratch_shapes=[
            pltpu.VMEM((3, 32, 128), F32),
            pltpu.VMEM((8, BOXES * PTS), F32),
            pltpu.VMEM((BOXES, 27), jnp.int32),
            pltpu.VMEM((RANK, BOXES * PTS), F32),
            pltpu.VMEM((BOXES, RANK, RANK), F32),
            pltpu.VMEM((9, 2, RANK, RANK), F32),
            pltpu.SemaphoreType.DMA((6,)),
            pltpu.VMEM((BOXES + REMOTE, 16, PTS), F32),
            pltpu.VMEM((BOXES, PTS, 48), BF16),
            pltpu.VMEM((BOXES + REMOTE, 48, PTS), BF16),
            pltpu.VMEM((BOXES + REMOTE, 32, 128), F32),
            pltpu.VMEM((BOXES + REMOTE, 8, PTS), F32),
            pltpu.VMEM((REMOTE, 8, PTS), F32),
            pltpu.VMEM((20, PTS, PTS), BF16),
            pltpu.VMEM((10, RANK, RANK), F32),
            pltpu.VMEM((9, RANK, RANK), F32),
            pltpu.VMEM((3, 3, 32, 128), F32),
            pltpu.VMEM((3, 7, 3, 32, 128), F32),
            *[pltpu.VMEM((RANK, 128), F32)] * 8,
            pltpu.SemaphoreType.DMA((4,)),
            pltpu.SemaphoreType.DMA((4,)),
            pltpu.SemaphoreType.DMA((4,)),
            pltpu.SemaphoreType.DMA((4,)),
            pltpu.SemaphoreType.DMA((21,)),
            pltpu.SemaphoreType.DMA((21,)),
        ],
        compiler_params=pltpu.CompilerParams(
            collective_id=0 if comm else None, has_side_effects=True, vmem_limit_bytes=62 * 2**20
        ),
        name="near_and_grams",
    )(points.reshape(3, 32, 128), probes, near_boxes, leaf_bases, box_transfer, upper_transfer)
    return pl.pallas_call(
        factor_kernel,
        out_shape=(
            jax.ShapeDtypeStruct((1, 1, 8, BOXES * PTS), F32),
            jax.ShapeDtypeStruct((1, 1, BOXES, RANK, RANK), F32),
            jax.ShapeDtypeStruct((1, 1, 10, RANK, RANK), F32),
        ),
        in_specs=[pl.BlockSpec(memory_space=pl.ANY)] * 3,
        out_specs=(pl.BlockSpec(memory_space=pl.ANY), vmem(), vmem()),
        scratch_shapes=[
            pltpu.VMEM((8, RANK, 128), F32),
            pltpu.VMEM((5, RANK, 128), F32),
            pltpu.VMEM((5, RANK, 128), F32),
            *[pltpu.VMEM((RANK, 128), F32)] * 5,
            pltpu.SemaphoreType.DMA((18,)),
        ],
        compiler_params=pltpu.CompilerParams(vmem_limit_bytes=62 * 2**20),
        name="factors",
    )(near, leaf, gram)


def solution(mesh):
    return jax.shard_map(
        functools.partial(on_device, (mesh.shape["ty"], mesh.shape["tx"]), True),
        mesh=mesh,
        in_specs=(
            P("ty", "tx", None, None),
            P("ty", "tx", None, None),
            P("ty", "tx", None, None),
            P("ty", "tx", None, None),
            P("ty", "tx", None, None, None),
            P(),
        ),
        out_specs=(
            P("ty", "tx", None, None),
            P("ty", "tx", None, None, None),
            P("ty", "tx", None, None, None),
        ),
        check_vma=False,
    )
```

```python
import functools
import math

import jax
import jax.numpy as jnp
from jax import lax
from jax.experimental import pallas as pl
from jax.experimental.pallas import tpu as pltpu
from jax.sharding import PartitionSpec as P

MESH = pl.DeviceIdType.MESH
HIGHEST = lax.Precision.HIGHEST
F32, BF16 = jnp.float32, jnp.bfloat16
LOG2E = 1.0 / math.log(2.0)
ALPHA = math.sqrt(3.0)
BOXES, PTS, RANK = 16, 256, 64
TEST_TY = 6
COLUMNS = ((0, 1), (0, 0), (1, 0), (1, 1))
BOX_AT = tuple(x + 2 * y + 4 * z for x, y in COLUMNS for z in range(4))
HALO = ((0, -1, 4, 8, 0), (-1, 0, 0, 8, 8), (-1, -1, 4, 4, 16), (-1, 1, 0, 4, 20))
REMOTE = 24
Z_PAIRS = tuple((a, b) for a in range(4) for b in range(4) if abs(a - b) <= 1)


def dot(a, b, ca, cb, precision=None):
    return lax.dot_general(
        a, b, (((ca,), (cb,)), ((), ())), precision=precision, preferred_element_type=F32
    )


def split3(value):
    high = value.astype(BF16).astype(F32)
    rest = value - high
    mid = rest.astype(BF16).astype(F32)
    return high, mid, (rest - mid).astype(BF16).astype(F32)


def features(rows, center, left):
    sub = lax.broadcasted_iota(jnp.int32, rows.shape, 0)
    cy, cx = center
    mid = jnp.where(sub == 0, cy, jnp.where(sub == 1, cx, 2.0))
    y = jnp.where(sub < 3, (rows - mid) * ALPHA, 0.0)
    norm = jnp.sum(y * y, axis=0, keepdims=True)
    zero = jnp.zeros_like(y)
    if left:
        h, m, l = split3(jnp.where(sub == 3, norm, y))
        one = jnp.where(sub == 4, 1.0, 0.0)
        coord = lambda v: jnp.where(sub < 3, -2.0 * v, 0.0)
        lead = lambda c, n: jnp.where(sub < 3, -2.0 * c, jnp.where(sub == 3, n, one))
        parts = (lead(h, h), lead(h, m), lead(m, l), coord(m), coord(h), coord(l))
    else:
        h, m, l = split3(jnp.where(sub == 4, norm, y))
        one = jnp.where(sub == 3, 1.0, 0.0)
        parts = (h + one, m + one, jnp.where(sub < 3, h, l) + one, m, l, h)
    return jnp.concatenate(parts, axis=0).astype(BF16)


def matern(square):
    s = jnp.maximum(square, 1e-12)
    c = s * lax.rsqrt(s)
    return ((1.0 + c) * jnp.exp2(c * -LOG2E)).astype(BF16)


def halves(packed):
    return jnp.concatenate([packed[:, :RANK], packed[:, RANK:]], axis=0)


def packed(full):
    return jnp.concatenate([full[:32], full[32:]], axis=1)


def remote(src, dst, send, recv, device, comm):
    if comm:
        return pltpu.make_async_remote_copy(
            src_ref=src, dst_ref=dst, send_sem=send, recv_sem=recv, device_id=device, device_id_type=MESH
        )
    return None


def main_kernel(sizes, comm, pts_in, prb_in, near_in, leaf_in, trans_in, upper_in,
                near_out, leaf_out, gram_out,
                pts, prb, near, leaf, trans, upper, loaded,
                box, left, right, mask, acc, back, kern, grams, paths, tree_out, tree_in,
                x0, x1, x2, x3, x4, x5, x6, x7,
                halo_send, halo_recv, back_send, back_recv, tree_send, tree_recv):
    xs = (x0, x1, x2, x3, x4, x5, x6, x7)
    loads = [
        pltpu.make_async_copy(src, dst, loaded.at[i])
        for i, (src, dst) in enumerate((
            (pts_in, pts), (prb_in.at[0, 0], prb), (near_in.at[0, 0], near),
            (leaf_in.at[0, 0], leaf), (trans_in.at[0, 0], trans), (upper_in, upper)))
    ]
    for load in loads:
        load.start()
    n_ty, n_tx = sizes
    ty, tx = (lax.axis_index("ty"), lax.axis_index("tx")) if comm else (jnp.int32(TEST_TY), jnp.int32(0))
    center = ((2 * ty + 1).astype(F32), (2 * tx + 1).astype(F32))

    def at(dy, dx):
        return (lax.rem(ty + dy + n_ty, n_ty), lax.rem(tx + dx + n_tx, n_tx))

    bits = [lax.rem(tx // 2**i, 2) for i in range(5)] + [lax.rem(ty // 2**i, 2) for i in range(4)]

    def relative(level, q):
        row, col = ty, tx
        for i in range(3):
            if q >> i & 1:
                b = level + i
                if b < 5:
                    col = col + 2**b * (1 - 2 * bits[b])
                else:
                    row = row + 2 ** (b - 5) * (1 - 2 * bits[b])
        return (row, col)

    peers = [at(*h[:2]) for h in HALO] + [at(-h[0], -h[1]) for h in HALO]
    peers += [relative(3 * r, q) for r in range(3) for q in range(1, 8)]
    if comm:
        barrier = pltpu.get_barrier_semaphore()
        for peer in peers:
            pl.semaphore_signal(barrier, inc=1, device_id=peer, device_id_type=MESH)

    z = ty // 2 + 3 * (1 - (ty * n_tx + tx + n_ty * n_tx - 1) // (n_ty * n_tx))
    near_z, first_z = 1 - z // 4, 1 - (z + 7) // 8
    pairs_ahead = near_z * (4 - z) - first_z

    @pl.when(ty == n_ty - 1)
    def _():
        box[24:40] = jnp.zeros((16, 16, PTS), F32)

    @pl.when(ty == 0)
    def _():
        back[8:24] = jnp.zeros((16, 8, PTS), F32)

    for load in loads[:3]:
        load.wait()
    for i, k in enumerate(BOX_AT):
        cols = slice(k * PTS, (k + 1) * PTS)
        for c in range(3):
            for h in range(2):
                box[i, c : c + 1, 128 * h : 128 * h + 128] = pts[c, 2 * k + h : 2 * k + h + 1, :]
        box[i, 8:16, :] = prb[:, cols]
        box[i, 3:8, :] = jnp.zeros((5, PTS), F32)
        box[i, 3:4, 0:27] = jnp.where(near[k : k + 1, :] >= 0, 1.0, 0.0)

    def halo(j):
        dy, dx, first, count, row = HALO[j]
        src, dst = box.at[pl.ds(first, count)], box.at[pl.ds(BOXES + row, count)]
        if comm:
            return pltpu.make_async_remote_copy(
                src_ref=src, dst_ref=dst, send_sem=halo_send.at[j], recv_sem=halo_recv.at[j],
                device_id=at(dy, dx), device_id_type=MESH)
        return pltpu.make_async_copy(src, dst, halo_recv.at[j])

    def reply(j):
        dy, dx, first, count, row = HALO[j]
        src, dst = acc.at[pl.ds(BOXES + row, count)], back.at[pl.ds(row, count)]
        if comm:
            return pltpu.make_async_remote_copy(
                src_ref=src, dst_ref=dst, send_sem=back_send.at[j], recv_sem=back_recv.at[j],
                device_id=at(-dy, -dx), device_id_type=MESH)
        return pltpu.make_async_copy(src, dst, back_recv.at[j])

    def exchange(r, q):
        count = 3 if q == 1 else 2 if q < 4 else 1
        src, dst = tree_out.at[r, pl.ds(0, count)], tree_in.at[r, q - 1, pl.ds(0, count)]
        j = 7 * r + q - 1
        if comm:
            return pltpu.make_async_remote_copy(
                src_ref=src, dst_ref=dst, send_sem=tree_send.at[j], recv_sem=tree_recv.at[j],
                device_id=relative(3 * r, q), device_id_type=MESH)
        return pltpu.make_async_copy(src, dst, tree_recv.at[j])

    def wait_send(copy):
        if comm:
            copy.wait_send()

    def wait_recv(copy):
        if comm:
            copy.wait_recv()
        else:
            copy.wait()

    for load in loads[3:]:
        load.wait()
    for r in range(3):
        path = None
        for i in range(3):
            step = upper[3 * r + i, bits[3 * r + i]]
            path = step if path is None else dot(path, step, 1, 0, HIGHEST)
            paths[3 * r + i] = path
    total = jnp.zeros((RANK, RANK), F32)
    pair = []
    for k in range(BOXES):
        v = leaf[:, k * PTS : (k + 1) * PTS]
        stack = jnp.concatenate(split3(v), axis=0).astype(BF16)
        c = dot(stack, stack, 1, 1)
        g = c[128:, :64] + c[:64, 128:] + c[64:128, 64:128]
        g = g + (c[:64, 64:128] + c[64:128, :64]) + c[:64, :64]
        pair.append(g)
        if k % 2:
            xs[k // 2][...] = jnp.concatenate(pair, axis=1)
            pair = []
        t = trans[k]
        total = total + dot(t, dot(g, t, 1, 0, HIGHEST), 0, 0, HIGHEST)
    grams[0] = total

    def send_round(r):
        node = grams[3 * r]
        for i in range(3):
            path = paths[3 * r + i]
            term = dot(path, dot(node, path, 1, 0, HIGHEST), 0, 0, HIGHEST)
            tree_out[r, 2 - i] = packed(term)
        for q in range(1, 8):
            exchange(r, q).start()

    def finish_round(r):
        for q in range(1, 8):
            wait_recv(exchange(r, q))
        for i in range(3):
            node = tree_out[r, 2 - i]
            for q in range(1, 2 ** (i + 1)):
                node = node + tree_in[r, q - 1, 2 - i]
            grams[3 * r + i + 1] = halves(node)

    lane = lax.broadcasted_iota(jnp.int32, (32, 128), 1)
    row = lax.broadcasted_iota(jnp.int32, (32, 128), 0)
    ones = jnp.ones((128, 128), BF16)
    diag = lax.broadcasted_iota(jnp.int32, (PTS, PTS), 0) == lax.broadcasted_iota(jnp.int32, (PTS, PTS), 1)
    eye = jnp.where(diag, 1.0, 0.0).astype(BF16)

    def prepare(i, own):
        rows = box[i, 0:8, :]
        right[i] = features(rows, center, False)
        if own:
            left[i] = dot(eye, features(rows, center, True), 1, 1).astype(BF16)
        slots = jnp.where(lane == row, box[i, 3:4, 0:128], 0.0).astype(BF16)
        mask[i] = dot(slots, ones, 1, 0)
        acc[i] = jnp.zeros((8, PTS), F32)

    def loop(n, body, unroll=1, first=0):
        lax.fori_loop(first, n, lambda i, c: (body(i), c)[1], 0, unroll=unroll)

    def probe(i, owner, slot):
        m = mask[owner, pl.ds(slot, 1), :]
        return (box[i, 8:16, :] * jnp.concatenate([m, m], axis=1)).astype(BF16)

    def factor(t):
        for p in range(8):
            factor_step(xs[p], leaf_out, p, 2 * t)

    def blocks(a0, b0, step, pairs, one_sided=(), steps=(), base=0):
        sums = {}

        def first(m, za, zb):
            kern[base + m] = matern(dot(left[a0 + za], right[b0 + zb], 1, 0))

        def add(key, value):
            sums[key] = value if key not in sums else sums[key] + value

        def second(m, za, zb):
            block = kern[base + m]
            a, b = a0 + za, b0 + zb
            slot = 13 + step + (zb - za)
            add(("a", za), dot(probe(b, a, slot), block, 1, 1))
            if (za, zb) not in one_sided:
                add(("b", zb), dot(probe(a, b, 26 - slot), block, 1, 0))

        late = 2
        for m in range(len(pairs) + late):
            if m % 5 == 1 and m // 5 < len(steps):
                factor(steps[m // 5])
            if m < len(pairs):
                first(m, *pairs[m])
            if m >= late:
                second(m - late, *pairs[m - late])
        for (side, z), value in sums.items():
            at_box = (a0 if side == "a" else b0) + z
            acc[at_box] = acc[at_box] + value

    loop(BOXES, lambda i: prepare(i, True), 4)

    def own_pair(i, base, begin):
        d, j = i // 2 + 1, lax.rem(i, 2)
        a = j * (1 + 1 // d)
        b = a + d - 2 * a * (d // 3)
        x = lambda p: p // 2
        y = lambda p: 1 - lax.rem((p + 1) // 2, 2)
        blocks(4 * a, 4 * b, 9 * (x(b) - x(a)) + 3 * (y(b) - y(a)), Z_PAIRS, base=base, steps=(begin + 2 * i, begin + 1 + 2 * i))

    def tx_pair(i, base=0):
        xa, xb = lax.rem(i, 2), i // 2
        blocks(12 * xa, BOXES + 4 * xb, 9 * (xb - xa) + 3, Z_PAIRS, base=base, steps=(done + 0 + 2 * i, done + 1 + 2 * i))

    def ty_pair(i, base=0):
        ya, p = lax.rem(i, 2), i // 2
        blocks(8 + 4 * ya, BOXES + 8 + 4 * p, 9 + 3 * (1 - p - ya), Z_PAIRS, base=base, steps=(done + 8 + 2 * i, done + 9 + 2 * i))

    def corner_pair(i, base=0):
        blocks(12 - 4 * i, BOXES + 16 + 4 * i, 9 + 3 * (1 - 2 * i), Z_PAIRS, base=base, steps=(done + 16 + 2 * i, done + 17 + 2 * i))

    def column(i, base=0):
        same = tuple((z, z) for z in range(4))
        blocks(4 * i, 4 * i, 0, same + ((0, 1), (1, 2), (2, 3)), same, base=base)

    def own_pairs(first, last, begin):
        loop(last, lambda i: (own_pair(2 * i, 0, begin), own_pair(2 * i + 1, 10, begin)), 1, first)

    own_pairs(0, pairs_ahead, 0)
    if comm:
        pl.semaphore_wait(barrier, len(peers))
    halo(0).start()

    @pl.when(ty > 0)
    def _():
        for j in range(1, 4):
            halo(j).start()

    send_round(0)
    loop(2, lambda i: (column(2 * i), column(2 * i + 1, 10)))
    wait_recv(halo(0))

    @pl.when(ty < n_ty - 1)
    def _():
        for j in range(1, 4):
            wait_recv(halo(j))

    loop(REMOTE, lambda i: prepare(BOXES + i, False), 4)
    done = 4 * pairs_ahead
    loop(2, lambda i: (tx_pair(2 * i), tx_pair(2 * i + 1, 10)))
    reply(0).start()
    finish_round(0)
    send_round(1)
    loop(2, lambda i: (ty_pair(2 * i), ty_pair(2 * i + 1, 10)))
    finish_round(1)
    send_round(2)
    loop(1, lambda i: (corner_pair(2 * i), corner_pair(2 * i + 1, 10)))

    @pl.when(ty < n_ty - 1)
    def _():
        for j in range(1, 4):
            reply(j).start()

    own_pairs(pairs_ahead, 3, 20)
    finish_round(2)
    for i in range(5):
        gram_out[i] = jnp.concatenate([grams[2 * i], grams[2 * i + 1]], axis=1)
    wait_recv(reply(0))

    @pl.when(ty > 0)
    def _():
        for j in range(1, 4):
            wait_recv(reply(j))

    for i in range(BOXES):
        value = acc[i]
        for dy, dx, start, count, at_row in HALO:
            if start <= i < start + count:
                value = value + back[at_row + i - start]
        near_out[i] = value
    wait_send(halo(0))
    wait_send(reply(0))

    @pl.when(ty > 0)
    def _():
        for j in range(1, 4):
            wait_send(halo(j))

    @pl.when(ty < n_ty - 1)
    def _():
        for j in range(1, 4):
            wait_send(reply(j))

    for r in range(3):
        for q in range(1, 8):
            wait_send(exchange(r, q))


def factor_step(x, out, p, j, top=0):
    lane = lax.broadcasted_iota(jnp.int32, (8, 128), 1)
    half = lane - lane % RANK
    i0, i1 = half + j, half + j + 1
    pick = lambda v, idx: jnp.take_along_axis(v, idx, axis=1)
    r0 = jnp.broadcast_to(x[pl.ds(j, 1), :], (8, 128))
    r1 = jnp.broadcast_to(x[pl.ds(j + 1, 1), :], (8, 128))
    a, b, c = pick(r0, i0), pick(r0, i1), pick(r1, i1)
    sa = lax.rsqrt(a)
    inv = sa * sa
    t = b * inv
    sc = lax.rsqrt(c - b * t)
    out0, out1 = r0 * sa, (r1 - t * r0) * sc
    out[p, pl.ds(j, 1), :] = out0[0:1]
    out[p, pl.ds(j + 1, 1), :] = out1[0:1]
    q1 = out1 * sc
    q0 = r0 * inv - t * q1
    for v in range(top, 8):
        rows = slice(8 * v, 8 * v + 8)
        old = x[rows, :]
        x[rows, :] = old - pick(old, i0) * q0 - pick(old, i1) * q1


def factor_kernel(near, leaf_in, gram_in, near_out, leaf_out, anc_out, leaf, gram, done, x0, x1, x2, x3, x4, sems):
    xs = (x0, x1, x2, x3, x4)
    copies = [pltpu.make_async_copy(gram_in, gram, sems.at[16]), pltpu.make_async_copy(leaf_in, leaf, sems.at[17])]
    for i, k in enumerate(BOX_AT):
        cols = pl.ds(k * PTS, PTS)
        copies.append(pltpu.make_async_copy(near.at[i], near_out.at[0, 0, :, cols], sems.at[i]))
    for copy in copies:
        copy.start()
    copies[0].wait()
    for p, x in enumerate(xs):
        x[...] = gram[p]
    r = lax.broadcasted_iota(jnp.int32, (RANK, RANK), 0)
    c = lax.broadcasted_iota(jnp.int32, (RANK, RANK), 1)
    triangle = lambda m, h: jnp.where(c >= r, m[:, RANK * h : RANK * (h + 1)], 0.0)
    copies[1].wait()
    for p in range(8):
        for h in range(2):
            leaf_out[0, 0, 2 * p + h] = triangle(leaf[p], h)
    for j in range(0, RANK, 2):
        for p, x in enumerate(xs):
            factor_step(x, done, p, j, j // 8)
    for p in range(5):
        for h in range(2):
            anc_out[0, 0, 2 * p + h] = triangle(done[p], h)
    for copy in copies[2:]:
        copy.wait()


def vmem():
    return pl.BlockSpec(memory_space=pltpu.VMEM)


def on_device(sizes, comm, points, probes, near_boxes, leaf_bases, box_transfer, upper_transfer):
    near, leaf, gram = pl.pallas_call(
        functools.partial(main_kernel, sizes, comm),
        out_shape=(
            jax.ShapeDtypeStruct((BOXES, 8, PTS), F32),
            jax.ShapeDtypeStruct((8, RANK, 128), F32),
            jax.ShapeDtypeStruct((5, RANK, 128), F32),
        ),
        in_specs=[pl.BlockSpec(memory_space=pl.ANY)] * 6,
        out_specs=(vmem(),) * 3,
        scratch_shapes=[
            pltpu.VMEM((3, 32, 128), F32),
            pltpu.VMEM((8, BOXES * PTS), F32),
            pltpu.VMEM((BOXES, 27), jnp.int32),
            pltpu.VMEM((RANK, BOXES * PTS), F32),
            pltpu.VMEM((BOXES, RANK, RANK), F32),
            pltpu.VMEM((9, 2, RANK, RANK), F32),
            pltpu.SemaphoreType.DMA((6,)),
            pltpu.VMEM((BOXES + REMOTE, 16, PTS), F32),
            pltpu.VMEM((BOXES, PTS, 48), BF16),
            pltpu.VMEM((BOXES + REMOTE, 48, PTS), BF16),
            pltpu.VMEM((BOXES + REMOTE, 32, 128), F32),
            pltpu.VMEM((BOXES + REMOTE, 8, PTS), F32),
            pltpu.VMEM((REMOTE, 8, PTS), F32),
            pltpu.VMEM((20, PTS, PTS), BF16),
            pltpu.VMEM((10, RANK, RANK), F32),
            pltpu.VMEM((9, RANK, RANK), F32),
            pltpu.VMEM((3, 3, 32, 128), F32),
            pltpu.VMEM((3, 7, 3, 32, 128), F32),
            *[pltpu.VMEM((RANK, 128), F32)] * 8,
            pltpu.SemaphoreType.DMA((4,)),
            pltpu.SemaphoreType.DMA((4,)),
            pltpu.SemaphoreType.DMA((4,)),
            pltpu.SemaphoreType.DMA((4,)),
            pltpu.SemaphoreType.DMA((21,)),
            pltpu.SemaphoreType.DMA((21,)),
        ],
        compiler_params=pltpu.CompilerParams(
            collective_id=0 if comm else None, has_side_effects=True, vmem_limit_bytes=62 * 2**20
        ),
        name="near_and_grams",
    )(points.reshape(3, 32, 128), probes, near_boxes, leaf_bases, box_transfer, upper_transfer)
    return pl.pallas_call(
        factor_kernel,
        out_shape=(
            jax.ShapeDtypeStruct((1, 1, 8, BOXES * PTS), F32),
            jax.ShapeDtypeStruct((1, 1, BOXES, RANK, RANK), F32),
            jax.ShapeDtypeStruct((1, 1, 10, RANK, RANK), F32),
        ),
        in_specs=[pl.BlockSpec(memory_space=pl.ANY)] * 3,
        out_specs=(pl.BlockSpec(memory_space=pl.ANY), vmem(), vmem()),
        scratch_shapes=[
            pltpu.VMEM((8, RANK, 128), F32),
            pltpu.VMEM((5, RANK, 128), F32),
            pltpu.VMEM((5, RANK, 128), F32),
            *[pltpu.VMEM((RANK, 128), F32)] * 5,
            pltpu.SemaphoreType.DMA((18,)),
        ],
        compiler_params=pltpu.CompilerParams(vmem_limit_bytes=62 * 2**20),
        name="factors",
    )(near, leaf, gram)


def solution(mesh):
    return jax.shard_map(
        functools.partial(on_device, (mesh.shape["ty"], mesh.shape["tx"]), True),
        mesh=mesh,
        in_specs=(
            P("ty", "tx", None, None),
            P("ty", "tx", None, None),
            P("ty", "tx", None, None),
            P("ty", "tx", None, None),
            P("ty", "tx", None, None, None),
            P(),
        ),
        out_specs=(
            P("ty", "tx", None, None),
            P("ty", "tx", None, None, None),
            P("ty", "tx", None, None, None),
        ),
        check_vma=False,
    )
```

```python
import functools
import math

import jax
import jax.numpy as jnp
from jax import lax
from jax.experimental import pallas as pl
from jax.experimental.pallas import tpu as pltpu
from jax.sharding import PartitionSpec as P

MESH = pl.DeviceIdType.MESH
HIGHEST = lax.Precision.HIGHEST
F32, BF16 = jnp.float32, jnp.bfloat16
LOG2E = 1.0 / math.log(2.0)
ALPHA = math.sqrt(3.0)
BOXES, PTS, RANK = 16, 256, 64
TEST_TY = 6
COLUMNS = ((0, 1), (0, 0), (1, 0), (1, 1))
BOX_AT = tuple(x + 2 * y + 4 * z for x, y in COLUMNS for z in range(4))
HALO = ((0, -1, 4, 8, 0), (-1, 0, 0, 8, 8), (-1, -1, 4, 4, 16), (-1, 1, 0, 4, 20))
REMOTE = 24
Z_PAIRS = tuple((a, b) for a in range(4) for b in range(4) if abs(a - b) <= 1)


def dot(a, b, ca, cb, precision=None):
    return lax.dot_general(
        a, b, (((ca,), (cb,)), ((), ())), precision=precision, preferred_element_type=F32
    )


def split3(value):
    high = value.astype(BF16).astype(F32)
    rest = value - high
    mid = rest.astype(BF16).astype(F32)
    return high, mid, (rest - mid).astype(BF16).astype(F32)


def features(rows, center, left):
    sub = lax.broadcasted_iota(jnp.int32, rows.shape, 0)
    cy, cx = center
    mid = jnp.where(sub == 0, cy, jnp.where(sub == 1, cx, 2.0))
    y = jnp.where(sub < 3, (rows - mid) * ALPHA, 0.0)
    norm = jnp.sum(y * y, axis=0, keepdims=True)
    zero = jnp.zeros_like(y)
    if left:
        h, m, l = split3(jnp.where(sub == 3, norm, y))
        one = jnp.where(sub == 4, 1.0, 0.0)
        coord = lambda v: jnp.where(sub < 3, -2.0 * v, 0.0)
        lead = lambda c, n: jnp.where(sub < 3, -2.0 * c, jnp.where(sub == 3, n, one))
        parts = (lead(h, h), lead(h, m), lead(m, l), coord(m), coord(h), coord(l))
    else:
        h, m, l = split3(jnp.where(sub == 4, norm, y))
        one = jnp.where(sub == 3, 1.0, 0.0)
        parts = (h + one, m + one, jnp.where(sub < 3, h, l) + one, m, l, h)
    return jnp.concatenate(parts, axis=0).astype(BF16)


def matern(square):
    s = jnp.maximum(square, 1e-12)
    c = s * lax.rsqrt(s)
    return ((1.0 + c) * jnp.exp2(c * -LOG2E)).astype(BF16)


def halves(packed):
    return jnp.concatenate([packed[:, :RANK], packed[:, RANK:]], axis=0)


def packed(full):
    return jnp.concatenate([full[:32], full[32:]], axis=1)


def remote(src, dst, send, recv, device, comm):
    if comm:
        return pltpu.make_async_remote_copy(
            src_ref=src, dst_ref=dst, send_sem=send, recv_sem=recv, device_id=device, device_id_type=MESH
        )
    return None


def main_kernel(sizes, comm, pts_in, prb_in, near_in, leaf_in, trans_in, upper_in,
                near_out, leaf_out, gram_out,
                pts, prb, near, leaf, trans, upper, loaded,
                box, left, right, mask, acc, back, kern, grams, paths, tree_out, tree_in,
                x0, x1, x2, x3, x4, x5, x6, x7,
                halo_send, halo_recv, back_send, back_recv, tree_send, tree_recv):
    xs = (x0, x1, x2, x3, x4, x5, x6, x7)
    loads = [
        pltpu.make_async_copy(src, dst, loaded.at[i])
        for i, (src, dst) in enumerate((
            (pts_in, pts), (prb_in.at[0, 0], prb), (near_in.at[0, 0], near),
            (leaf_in.at[0, 0], leaf), (trans_in.at[0, 0], trans), (upper_in, upper)))
    ]
    for load in loads:
        load.start()
    n_ty, n_tx = sizes
    ty, tx = (lax.axis_index("ty"), lax.axis_index("tx")) if comm else (jnp.int32(TEST_TY), jnp.int32(0))
    center = ((2 * ty + 1).astype(F32), (2 * tx + 1).astype(F32))

    def at(dy, dx):
        return (lax.rem(ty + dy + n_ty, n_ty), lax.rem(tx + dx + n_tx, n_tx))

    bits = [lax.rem(tx // 2**i, 2) for i in range(5)] + [lax.rem(ty // 2**i, 2) for i in range(4)]

    def relative(level, q):
        row, col = ty, tx
        for i in range(3):
            if q >> i & 1:
                b = level + i
                if b < 5:
                    col = col + 2**b * (1 - 2 * bits[b])
                else:
                    row = row + 2 ** (b - 5) * (1 - 2 * bits[b])
        return (row, col)

    peers = [at(*h[:2]) for h in HALO] + [at(-h[0], -h[1]) for h in HALO]
    peers += [relative(3 * r, q) for r in range(3) for q in range(1, 8)]
    if comm:
        barrier = pltpu.get_barrier_semaphore()
        for peer in peers:
            pl.semaphore_signal(barrier, inc=1, device_id=peer, device_id_type=MESH)

    z = ty // 2 + 3 * (1 - (ty * n_tx + tx + n_ty * n_tx - 1) // (n_ty * n_tx))
    near_z, first_z = 1 - z // 4, 1 - (z + 7) // 8
    pairs_ahead = near_z * (4 - z) - first_z

    @pl.when(ty == n_ty - 1)
    def _():
        box[24:40] = jnp.zeros((16, 16, PTS), F32)

    @pl.when(ty == 0)
    def _():
        back[8:24] = jnp.zeros((16, 8, PTS), F32)

    for load in loads[:3]:
        load.wait()
    for i, k in enumerate(BOX_AT):
        cols = slice(k * PTS, (k + 1) * PTS)
        for c in range(3):
            for h in range(2):
                box[i, c : c + 1, 128 * h : 128 * h + 128] = pts[c, 2 * k + h : 2 * k + h + 1, :]
        box[i, 8:16, :] = prb[:, cols]
        box[i, 3:8, :] = jnp.zeros((5, PTS), F32)
        box[i, 3:4, 0:27] = jnp.where(near[k : k + 1, :] >= 0, 1.0, 0.0)

    def halo(j):
        dy, dx, first, count, row = HALO[j]
        src, dst = box.at[pl.ds(first, count)], box.at[pl.ds(BOXES + row, count)]
        if comm:
            return pltpu.make_async_remote_copy(
                src_ref=src, dst_ref=dst, send_sem=halo_send.at[j], recv_sem=halo_recv.at[j],
                device_id=at(dy, dx), device_id_type=MESH)
        return pltpu.make_async_copy(src, dst, halo_recv.at[j])

    def reply(j):
        dy, dx, first, count, row = HALO[j]
        src, dst = acc.at[pl.ds(BOXES + row, count)], back.at[pl.ds(row, count)]
        if comm:
            return pltpu.make_async_remote_copy(
                src_ref=src, dst_ref=dst, send_sem=back_send.at[j], recv_sem=back_recv.at[j],
                device_id=at(-dy, -dx), device_id_type=MESH)
        return pltpu.make_async_copy(src, dst, back_recv.at[j])

    def exchange(r, q):
        count = 3 if q == 1 else 2 if q < 4 else 1
        src, dst = tree_out.at[r, pl.ds(0, count)], tree_in.at[r, q - 1, pl.ds(0, count)]
        j = 7 * r + q - 1
        if comm:
            return pltpu.make_async_remote_copy(
                src_ref=src, dst_ref=dst, send_sem=tree_send.at[j], recv_sem=tree_recv.at[j],
                device_id=relative(3 * r, q), device_id_type=MESH)
        return pltpu.make_async_copy(src, dst, tree_recv.at[j])

    def wait_send(copy):
        if comm:
            copy.wait_send()

    def wait_recv(copy):
        if comm:
            copy.wait_recv()
        else:
            copy.wait()

    for load in loads[3:]:
        load.wait()
    for r in range(3):
        path = None
        for i in range(3):
            step = upper[3 * r + i, bits[3 * r + i]]
            path = step if path is None else dot(path, step, 1, 0, HIGHEST)
            paths[3 * r + i] = path
    total = jnp.zeros((RANK, RANK), F32)
    pair = []
    for k in range(BOXES):
        v = leaf[:, k * PTS : (k + 1) * PTS]
        stack = jnp.concatenate(split3(v), axis=0).astype(BF16)
        c = dot(stack, stack, 1, 1)
        g = c[128:, :64] + c[:64, 128:] + c[64:128, 64:128]
        g = g + (c[:64, 64:128] + c[64:128, :64]) + c[:64, :64]
        pair.append(g)
        if k % 2:
            xs[k // 2][...] = jnp.concatenate(pair, axis=1)
            pair = []
        t = trans[k]
        total = total + dot(t, dot(g, t, 1, 0, HIGHEST), 0, 0, HIGHEST)
    grams[0] = total

    def send_round(r):
        node = grams[3 * r]
        for i in range(3):
            path = paths[3 * r + i]
            term = dot(path, dot(node, path, 1, 0, HIGHEST), 0, 0, HIGHEST)
            tree_out[r, 2 - i] = packed(term)
        for q in range(1, 8):
            exchange(r, q).start()

    def finish_round(r):
        for q in range(1, 8):
            wait_recv(exchange(r, q))
        for i in range(3):
            node = tree_out[r, 2 - i]
            for q in range(1, 2 ** (i + 1)):
                node = node + tree_in[r, q - 1, 2 - i]
            grams[3 * r + i + 1] = halves(node)

    lane = lax.broadcasted_iota(jnp.int32, (32, 128), 1)
    row = lax.broadcasted_iota(jnp.int32, (32, 128), 0)
    ones = jnp.ones((128, 128), BF16)
    diag = lax.broadcasted_iota(jnp.int32, (PTS, PTS), 0) == lax.broadcasted_iota(jnp.int32, (PTS, PTS), 1)
    eye = jnp.where(diag, 1.0, 0.0).astype(BF16)

    def prepare(i, own):
        rows = box[i, 0:8, :]
        right[i] = features(rows, center, False)
        if own:
            left[i] = dot(eye, features(rows, center, True), 1, 1).astype(BF16)
        slots = jnp.where(lane == row, box[i, 3:4, 0:128], 0.0).astype(BF16)
        mask[i] = dot(slots, ones, 1, 0)
        acc[i] = jnp.zeros((8, PTS), F32)

    def loop(n, body, unroll=1, first=0):
        lax.fori_loop(first, n, lambda i, c: (body(i), c)[1], 0, unroll=unroll)

    def probe(i, owner, slot):
        m = mask[owner, pl.ds(slot, 1), :]
        return (box[i, 8:16, :] * jnp.concatenate([m, m], axis=1)).astype(BF16)

    def factor(t):
        for p in range(8):
            factor_step(xs[p], leaf_out, p, 2 * t)

    def blocks(a0, b0, step, pairs, one_sided=(), steps=(), base=0):
        sums = {}

        def first(m, za, zb):
            kern[base + m] = matern(dot(left[a0 + za], right[b0 + zb], 1, 0))

        def add(key, value):
            sums[key] = value if key not in sums else sums[key] + value

        def second(m, za, zb):
            block = kern[base + m]
            a, b = a0 + za, b0 + zb
            slot = 13 + step + (zb - za)
            add(("a", za), dot(probe(b, a, slot), block, 1, 1))
            if (za, zb) not in one_sided:
                add(("b", zb), dot(probe(a, b, 26 - slot), block, 1, 0))

        late = 2
        for m in range(len(pairs) + late):
            if m % 5 == 1 and m // 5 < len(steps):
                factor(steps[m // 5])
            if m < len(pairs):
                first(m, *pairs[m])
            if m >= late:
                second(m - late, *pairs[m - late])
        for (side, z), value in sums.items():
            at_box = (a0 if side == "a" else b0) + z
            acc[at_box] = acc[at_box] + value

    loop(BOXES, lambda i: prepare(i, True), 4)

    def own_pair(i, base, begin):
        d, j = i // 2 + 1, lax.rem(i, 2)
        a = j * (1 + 1 // d)
        b = a + d - 2 * a * (d // 3)
        x = lambda p: p // 2
        y = lambda p: 1 - lax.rem((p + 1) // 2, 2)
        blocks(4 * a, 4 * b, 9 * (x(b) - x(a)) + 3 * (y(b) - y(a)), Z_PAIRS, base=base, steps=(begin + 2 * i, begin + 1 + 2 * i))

    def tx_pair(i, base=0):
        xa, xb = lax.rem(i, 2), i // 2
        blocks(12 * xa, BOXES + 4 * xb, 9 * (xb - xa) + 3, Z_PAIRS, base=base, steps=(done + 0 + 2 * i, done + 1 + 2 * i))

    def ty_pair(i, base=0):
        ya, p = lax.rem(i, 2), i // 2
        blocks(8 + 4 * ya, BOXES + 8 + 4 * p, 9 + 3 * (1 - p - ya), Z_PAIRS, base=base, steps=(done + 8 + 2 * i, done + 9 + 2 * i))

    def corner_pair(i, base=0):
        blocks(12 - 4 * i, BOXES + 16 + 4 * i, 9 + 3 * (1 - 2 * i), Z_PAIRS, base=base, steps=(done + 16 + 2 * i, done + 17 + 2 * i))

    def column(i, base=0):
        same = tuple((z, z) for z in range(4))
        blocks(4 * i, 4 * i, 0, same + ((0, 1), (1, 2), (2, 3)), same, base=base)

    def own_pairs(first, last, begin):
        loop(last, lambda i: (own_pair(2 * i, 0, begin), own_pair(2 * i + 1, 10, begin)), 1, first)

    own_pairs(0, pairs_ahead, 0)
    if comm:
        pl.semaphore_wait(barrier, len(peers))
    send_round(0)
    halo(0).start()

    @pl.when(ty > 0)
    def _():
        for j in range(1, 4):
            halo(j).start()

    loop(2, lambda i: (column(2 * i), column(2 * i + 1, 10)))
    finish_round(0)
    send_round(1)
    wait_recv(halo(0))

    @pl.when(ty < n_ty - 1)
    def _():
        for j in range(1, 4):
            wait_recv(halo(j))

    loop(REMOTE, lambda i: prepare(BOXES + i, False), 4)
    done = 4 * pairs_ahead
    loop(2, lambda i: (tx_pair(2 * i), tx_pair(2 * i + 1, 10)))
    finish_round(1)
    send_round(2)
    reply(0).start()
    loop(2, lambda i: (ty_pair(2 * i), ty_pair(2 * i + 1, 10)))
    loop(1, lambda i: (corner_pair(2 * i), corner_pair(2 * i + 1, 10)))

    @pl.when(ty < n_ty - 1)
    def _():
        for j in range(1, 4):
            reply(j).start()

    own_pairs(pairs_ahead, 3, 20)
    wait_recv(reply(0))

    @pl.when(ty > 0)
    def _():
        for j in range(1, 4):
            wait_recv(reply(j))

    for i in range(BOXES):
        value = acc[i]
        for dy, dx, start, count, at_row in HALO:
            if start <= i < start + count:
                value = value + back[at_row + i - start]
        near_out[i] = value
    finish_round(2)
    for i in range(5):
        gram_out[i] = jnp.concatenate([grams[2 * i], grams[2 * i + 1]], axis=1)
    wait_send(halo(0))
    wait_send(reply(0))

    @pl.when(ty > 0)
    def _():
        for j in range(1, 4):
            wait_send(halo(j))

    @pl.when(ty < n_ty - 1)
    def _():
        for j in range(1, 4):
            wait_send(reply(j))

    for r in range(3):
        for q in range(1, 8):
            wait_send(exchange(r, q))


def factor_step(x, out, p, j, top=0):
    lane = lax.broadcasted_iota(jnp.int32, (8, 128), 1)
    half = lane - lane % RANK
    i0, i1 = half + j, half + j + 1
    pick = lambda v, idx: jnp.take_along_axis(v, idx, axis=1)
    r0 = jnp.broadcast_to(x[pl.ds(j, 1), :], (8, 128))
    r1 = jnp.broadcast_to(x[pl.ds(j + 1, 1), :], (8, 128))
    a, b, c = pick(r0, i0), pick(r0, i1), pick(r1, i1)
    sa = lax.rsqrt(a)
    inv = sa * sa
    t = b * inv
    sc = lax.rsqrt(c - b * t)
    out0, out1 = r0 * sa, (r1 - t * r0) * sc
    out[p, pl.ds(j, 1), :] = out0[0:1]
    out[p, pl.ds(j + 1, 1), :] = out1[0:1]
    q1 = out1 * sc
    q0 = r0 * inv - t * q1
    for v in range(top, 8):
        rows = slice(8 * v, 8 * v + 8)
        old = x[rows, :]
        x[rows, :] = old - pick(old, i0) * q0 - pick(old, i1) * q1


def factor_kernel(near, leaf_in, gram_in, near_out, leaf_out, anc_out, leaf, gram, done, x0, x1, x2, x3, x4, sems):
    xs = (x0, x1, x2, x3, x4)
    copies = [pltpu.make_async_copy(gram_in, gram, sems.at[16]), pltpu.make_async_copy(leaf_in, leaf, sems.at[17])]
    for i, k in enumerate(BOX_AT):
        cols = pl.ds(k * PTS, PTS)
        copies.append(pltpu.make_async_copy(near.at[i], near_out.at[0, 0, :, cols], sems.at[i]))
    for copy in copies:
        copy.start()
    copies[0].wait()
    for p, x in enumerate(xs):
        x[...] = gram[p]
    r = lax.broadcasted_iota(jnp.int32, (RANK, RANK), 0)
    c = lax.broadcasted_iota(jnp.int32, (RANK, RANK), 1)
    triangle = lambda m, h: jnp.where(c >= r, m[:, RANK * h : RANK * (h + 1)], 0.0)
    copies[1].wait()
    for p in range(8):
        for h in range(2):
            leaf_out[0, 0, 2 * p + h] = triangle(leaf[p], h)
    for j in range(0, RANK, 2):
        for p, x in enumerate(xs):
            factor_step(x, done, p, j, j // 8)
    for p in range(5):
        for h in range(2):
            anc_out[0, 0, 2 * p + h] = triangle(done[p], h)
    for copy in copies[2:]:
        copy.wait()


def vmem():
    return pl.BlockSpec(memory_space=pltpu.VMEM)


def on_device(sizes, comm, points, probes, near_boxes, leaf_bases, box_transfer, upper_transfer):
    near, leaf, gram = pl.pallas_call(
        functools.partial(main_kernel, sizes, comm),
        out_shape=(
            jax.ShapeDtypeStruct((BOXES, 8, PTS), F32),
            jax.ShapeDtypeStruct((8, RANK, 128), F32),
            jax.ShapeDtypeStruct((5, RANK, 128), F32),
        ),
        in_specs=[pl.BlockSpec(memory_space=pl.ANY)] * 6,
        out_specs=(vmem(),) * 3,
        scratch_shapes=[
            pltpu.VMEM((3, 32, 128), F32),
            pltpu.VMEM((8, BOXES * PTS), F32),
            pltpu.VMEM((BOXES, 27), jnp.int32),
            pltpu.VMEM((RANK, BOXES * PTS), F32),
            pltpu.VMEM((BOXES, RANK, RANK), F32),
            pltpu.VMEM((9, 2, RANK, RANK), F32),
            pltpu.SemaphoreType.DMA((6,)),
            pltpu.VMEM((BOXES + REMOTE, 16, PTS), F32),
            pltpu.VMEM((BOXES, PTS, 48), BF16),
            pltpu.VMEM((BOXES + REMOTE, 48, PTS), BF16),
            pltpu.VMEM((BOXES + REMOTE, 32, 128), F32),
            pltpu.VMEM((BOXES + REMOTE, 8, PTS), F32),
            pltpu.VMEM((REMOTE, 8, PTS), F32),
            pltpu.VMEM((20, PTS, PTS), BF16),
            pltpu.VMEM((10, RANK, RANK), F32),
            pltpu.VMEM((9, RANK, RANK), F32),
            pltpu.VMEM((3, 3, 32, 128), F32),
            pltpu.VMEM((3, 7, 3, 32, 128), F32),
            *[pltpu.VMEM((RANK, 128), F32)] * 8,
            pltpu.SemaphoreType.DMA((4,)),
            pltpu.SemaphoreType.DMA((4,)),
            pltpu.SemaphoreType.DMA((4,)),
            pltpu.SemaphoreType.DMA((4,)),
            pltpu.SemaphoreType.DMA((21,)),
            pltpu.SemaphoreType.DMA((21,)),
        ],
        compiler_params=pltpu.CompilerParams(
            collective_id=0 if comm else None, has_side_effects=True, vmem_limit_bytes=62 * 2**20
        ),
        name="near_and_grams",
    )(points.reshape(3, 32, 128), probes, near_boxes, leaf_bases, box_transfer, upper_transfer)
    return pl.pallas_call(
        factor_kernel,
        out_shape=(
            jax.ShapeDtypeStruct((1, 1, 8, BOXES * PTS), F32),
            jax.ShapeDtypeStruct((1, 1, BOXES, RANK, RANK), F32),
            jax.ShapeDtypeStruct((1, 1, 10, RANK, RANK), F32),
        ),
        in_specs=[pl.BlockSpec(memory_space=pl.ANY)] * 3,
        out_specs=(pl.BlockSpec(memory_space=pl.ANY), vmem(), vmem()),
        scratch_shapes=[
            pltpu.VMEM((8, RANK, 128), F32),
            pltpu.VMEM((5, RANK, 128), F32),
            pltpu.VMEM((5, RANK, 128), F32),
            *[pltpu.VMEM((RANK, 128), F32)] * 5,
            pltpu.SemaphoreType.DMA((18,)),
        ],
        compiler_params=pltpu.CompilerParams(vmem_limit_bytes=62 * 2**20),
        name="factors",
    )(near, leaf, gram)


def solution(mesh):
    return jax.shard_map(
        functools.partial(on_device, (mesh.shape["ty"], mesh.shape["tx"]), True),
        mesh=mesh,
        in_specs=(
            P("ty", "tx", None, None),
            P("ty", "tx", None, None),
            P("ty", "tx", None, None),
            P("ty", "tx", None, None),
            P("ty", "tx", None, None, None),
            P(),
        ),
        out_specs=(
            P("ty", "tx", None, None),
            P("ty", "tx", None, None, None),
            P("ty", "tx", None, None, None),
        ),
        check_vma=False,
    )
```
